128 devices in a mesh: prompt: 4 (over x), sample: 32 (over y, z, core).
Axes of the slice: x: 4, y: 4, z: 4, core: 2. Of those that a mesh axis runs over, the one named last changes fastest.
Arguments:
- embeddings: bfloat16 [128, 512, 1024], P(('prompt', 'sample')), parts along dimension 0
- lengths: int32 [128], P(('prompt', 'sample')), parts along dimension 0, may hold values from 32 to 512, as said below
Outputs:
- precision: float32 [128, 32], P(('prompt', 'sample')), parts along dimension 0
- utility: float32 [128], P(('prompt', 'sample')), parts along dimension 0
The draws below stay inside these ranges and needn't reach their ends.
There are 4 independent parts, one for each index of `prompt`. The reference program is written for one: setup_inputs(seed, part) draws one part's arguments, and reference() takes and returns one part's arrays. A program takes and returns all parts, laid end to end along the dimension named above; each array names one. Nothing has to cross between parts.
Inputs may be any that keep to these rules, and one draw needn't show every extreme that they name: `lengths`: some sample of the prompt has exactly 512 tokens.
All inputs are finite; a program needn't handle non-finite values.
Results may differ from the reference program's by a relative error of at most 0.0007.
Values may be sent and summed in bfloat16 or wider, within the bound.
No kernel may reach another device: no remote copies, remote signals or barrier semaphores. Data moves between devices by JAX's collectives and lax.ppermute only.
A program may use at most 128 MiB of HBM per device.

```python
import jax
import jax.numpy as jnp
from jax import lax

E = 1024
LEN = 512
SAMPLES = 32


def draw_embeddings(key, part):
    keys = jax.random.split(jax.random.fold_in(key, 11), 4)
    pool = jax.random.normal(keys[0], (256, E), jnp.float32)
    offset = jax.random.randint(keys[1], (SAMPLES, 1), 0, 160)
    concept = offset + jax.random.randint(keys[2], (SAMPLES, LEN), 0, 96)
    centre = jnp.take(pool, concept, axis=0)
    noise = jax.random.normal(keys[3], (SAMPLES, LEN, E), jnp.float32)
    result = centre + 0.6 * noise
    return result.astype(jnp.bfloat16)


def draw_lengths(key, part):
    keys = jax.random.split(jax.random.fold_in(key, 23), 2)
    drawn = jax.random.randint(keys[0], (SAMPLES,), max(1, LEN // 16), LEN + 1)
    chosen = jax.random.randint(keys[1], (), 0, SAMPLES)
    return jnp.where(jnp.arange(SAMPLES) == chosen, LEN, drawn).astype(jnp.int32)


def setup_inputs(seed: int = 0, part: int = 0) -> dict:
    arg_keys = jax.random.split(jax.random.key(seed), 3)
    part_splits = jax.random.split(jax.random.fold_in(arg_keys[2], part), 3)
    return {
        "embeddings": draw_embeddings(jax.random.fold_in(jax.random.fold_in(arg_keys[2], part), 71), part),
        "lengths": draw_lengths(jax.random.fold_in(jax.random.fold_in(arg_keys[2], part), 71), part),
    }


def reference(embeddings, lengths):
    values = embeddings.astype(jnp.float32)
    unit = (values / jnp.sqrt(lax.optimization_barrier(jnp.sum(values * values, axis=2, keepdims=True)) + 1e-06)).astype(jnp.bfloat16)
    flat = unit.reshape(SAMPLES * LEN, E)
    places = jnp.arange(LEN, dtype=jnp.int32)
    valid = places[None, :] < lengths[:, None]

    def one_row(items):
        own, own_len = items
        similar = jnp.dot(own, flat.T, preferred_element_type=jnp.float32).reshape(LEN, SAMPLES, LEN)
        masked = jnp.where(valid[None, :, :], similar, jnp.float32(-4.0))
        best = lax.optimization_barrier(jnp.max(masked, axis=2))
        keep = places[:, None] < own_len
        return lax.optimization_barrier(jnp.sum(jnp.where(keep, best, jnp.float32(0.0)), axis=0)) / own_len.astype(jnp.float32)
    precision = lax.map(one_row, (unit, lengths))
    both = precision + precision.T
    offdiag = jnp.arange(SAMPLES)[:, None] != jnp.arange(SAMPLES)[None, :]
    utility = lax.optimization_barrier(jnp.sum(jnp.where(offdiag, both, jnp.float32(0.0)), axis=1)) / jnp.float32(2 * (SAMPLES - 1))
    return (precision, utility)
```

```python
import functools

import jax
import jax.numpy as jnp
import numpy as np
from jax import lax
from jax.experimental import pallas as pl
from jax.experimental.pallas import tpu as pltpu
from jax.sharding import PartitionSpec as P

N = 4
HALF = 256
TAG = 16


def device(y, z, core):
    return ((y % N) * N + z % N) * 2 + core % 2


def moves(dy, dz, dcore=0, flip=False):
    pairs = []
    for y in range(N):
        for z in range(N):
            for core in range(2):
                change = dcore + (1 if flip and (y + dy) % N >= N // 2 else 0)
                pairs.append((device(y, z, core), device(y + dy, z + dz, core + change)))
    return pairs


def shift(x, dy, dz, dcore=0, flip=False):
    return lax.ppermute(x, "sample", moves(dy, dz, dcore, flip))


def plan(here):
    y, z, core = here // (2 * N), here // 2 % N, here % 2
    low, left = int(y >= N // 2), int(z >= N // 2)

    def at(dy, dz, flip=0):
        return device(y + dy, z + dz, core + flip)

    own, sib, up, up_o, right, right_o = at(0, 0), at(0, 0, 1), at(1, 0), at(1, 0, 1), at(0, 1), at(0, 1, 1)
    far_y, far_z = at(2, 0), at(0, 2, low)
    columns = [
        (0, 0, own, own, 1, 0, 0),
        (0, 1, own, sib, 0, 2, 0),
        (2, 0, up, own, 3, 1, 1),
        (2, 1, up, sib, 0, 2, 1),
        (5, 0, right, own, 6, 0, 1),
        (5, 1, right, sib, 0, 0, 1),
        (2, 5, up, right, 0, 0, 1),
        (2, 6, up, right_o, 0, 7, 1),
        (4, 5, at(-1, 0), right, 5, 0, 1),
        (4, 6, at(-1, 0), right_o, 0, 0, 1),
        (7, 5 + left, at(0, -1), at(0, 1, left), 8, 0, 1),
        (4, 2 + low, at(-1, 0), at(1, 0, low), 0, 4, 1),
        (0, 4, far_y, right, 1, 5, 1),
        (0, 5, far_y, right_o, 0, 6, 1),
        (1, 2, far_z, up, 2, 3, 1),
        (1, 3, far_z, up_o, 0, 4, 1),
        (0, 1, far_y, far_z, 0, 0, 1),
    ]
    return np.array(columns, np.int32).T


def unit_kernel(len_ref, emb_ref, head_ref, tail_ref):
    length = len_ref[0]
    first = None
    for start, out in ((0, head_ref), (HALF, tail_ref)):
        values = emb_ref[0, start : start + HALF, :].astype(jnp.float32)
        norm = jnp.sqrt(jnp.sum(values * values, axis=1, keepdims=True) + 1e-06)
        unit = values / norm
        if first is None:
            first = unit[0:1, :]
        places = lax.broadcasted_iota(jnp.int32, (HALF, 1), 0) + start
        out[0:HALF, :] = jnp.where(places < length, unit, first).astype(jnp.bfloat16)
    rows = lax.broadcasted_iota(jnp.int32, (TAG, head_ref.shape[1]), 0)
    tag = jnp.where(rows < TAG // 2, length // 16, length % 16)
    head_ref[HALF : HALF + TAG, :] = tag.astype(jnp.float32).astype(jnp.bfloat16)


def make_unit(lengths, embeddings):
    width = embeddings.shape[2]
    return pl.pallas_call(
        unit_kernel,
        out_shape=(
            jax.ShapeDtypeStruct((HALF + TAG, width), jnp.bfloat16),
            jax.ShapeDtypeStruct((HALF, width), jnp.bfloat16),
        ),
        in_specs=[
            pl.BlockSpec(memory_space=pltpu.SMEM),
            pl.BlockSpec(memory_space=pltpu.VMEM),
        ],
        out_specs=(
            pl.BlockSpec(memory_space=pltpu.VMEM),
            pl.BlockSpec(memory_space=pltpu.VMEM),
        ),
        compiler_params=pltpu.CompilerParams(vmem_limit_bytes=24 * 2**20),
        name="unit",
    )(lengths, embeddings)


def pairs_kernel(slots, base, count, tab_ref, before_ref, *refs):
    ins = refs[: 2 * slots]
    out_ref, tok, tag, sem = refs[2 * slots :]
    for s in range(slots):
        head, tail = ins[2 * s], ins[2 * s + 1]
        for c in (
            pltpu.make_async_copy(head.at[0:HALF, :], tok.at[s, 0:HALF, :], sem.at[s, 0]),
            pltpu.make_async_copy(tail.at[:, :], tok.at[s, HALF : 2 * HALF, :], sem.at[s, 1]),
            pltpu.make_async_copy(head.at[HALF : HALF + TAG, 0:128], tag.at[s], sem.at[s, 2]),
        ):
            c.start()

    def arrive(s):
        pltpu.make_async_copy(ins[0].at[0:HALF, :], tok.at[s, 0:HALF, :], sem.at[s, 0]).wait()
        pltpu.make_async_copy(ins[1].at[:, :], tok.at[s, HALF : 2 * HALF, :], sem.at[s, 1]).wait()
        pltpu.make_async_copy(
            ins[0].at[HALF : HALF + TAG, 0:128], tag.at[s], sem.at[s, 2]
        ).wait()

    out_ref[...] = before_ref[...]
    owners = lax.broadcasted_iota(jnp.int32, out_ref.shape, 0)
    lanes = lax.broadcasted_iota(jnp.int32, out_ref.shape, 1)
    total = out_ref.shape[0]

    def length_of(s):
        value = tag[s].astype(jnp.float32)
        return (
            jnp.max(value[0 : TAG // 2]).astype(jnp.int32) * 16
            + jnp.max(value[TAG // 2 : TAG]).astype(jnp.int32)
        )

    @pl.loop(base, base + count)
    def _(k):
        u, v = tab_ref[0, k], tab_ref[1, k]

        for wait in (4, 5):

            @pl.when(tab_ref[wait, k] > 0)
            def _():
                arrive(tab_ref[wait, k] - 1)

        len_u, len_v = length_of(u), length_of(v)
        own, other = tab_ref[2, k], tab_ref[3, k]
        both = tab_ref[6, k]

        def score(rows, cols):
            right = tok[v, 0:cols, :]
            best_col = None
            ahead = jnp.zeros((1, 1), jnp.float32)
            for start in range(0, rows, HALF):
                similar = lax.dot_general(
                    tok[u, start : start + HALF, :],
                    right,
                    (((1,), (1,)), ((), ())),
                    preferred_element_type=jnp.float32,
                )
                best_row = jnp.max(similar, axis=1, keepdims=True)
                col = jnp.max(similar, axis=0, keepdims=True)
                best_col = col if best_col is None else jnp.maximum(best_col, col)
                places = lax.broadcasted_iota(jnp.int32, (HALF, 1), 0) + start
                ahead += jnp.sum(
                    jnp.where(places < len_u, best_row, 0.0), axis=0, keepdims=True
                )
            places = lax.broadcasted_iota(jnp.int32, (1, cols), 1)
            behind = jnp.sum(jnp.where(places < len_v, best_col, 0.0), axis=1, keepdims=True)
            ahead = ahead / len_u.astype(jnp.float32)
            behind = behind / len_v.astype(jnp.float32)
            at_u = owners == own
            at_v = (owners == other) & (both == 1)
            fore = (at_u & (lanes == other)) | (at_v & (lanes == total + own))
            back = (at_u & (lanes == total + other)) | (at_v & (lanes == own))
            out_ref[...] += jnp.where(fore, ahead, 0.0) + jnp.where(back, behind, 0.0)

        long_u, long_v = len_u > HALF, len_v > HALF
        for bu in (False, True):
            for bv in (False, True):

                @pl.when((long_u == bu) & (long_v == bv))
                def _():
                    score(2 * HALF if bu else HALF, 2 * HALF if bv else HALF)


def run_pairs(table, base, count, before, blocks, name):
    slots = len(blocks)
    width = blocks[0][0].shape[1]
    flops = 2 * count * (2 * HALF) ** 2 * width
    return pl.pallas_call(
        functools.partial(pairs_kernel, slots, base, count),
        out_shape=jax.ShapeDtypeStruct(before.shape, jnp.float32),
        in_specs=[
            pl.BlockSpec(memory_space=pltpu.SMEM),
            pl.BlockSpec(memory_space=pltpu.VMEM),
        ]
        + [pl.BlockSpec(memory_space=pl.ANY)] * (2 * slots),
        out_specs=pl.BlockSpec(memory_space=pltpu.VMEM),
        scratch_shapes=[
            pltpu.VMEM((slots, 2 * HALF, width), jnp.bfloat16),
            pltpu.VMEM((slots, TAG, 128), jnp.bfloat16),
            pltpu.SemaphoreType.DMA((slots, 3)),
        ],
        compiler_params=pltpu.CompilerParams(vmem_limit_bytes=40 * 2**20),
        cost_estimate=pl.CostEstimate(
            flops=flops, bytes_accessed=slots * 2 * 2 * HALF * width, transcendentals=0
        ),
        name=name,
    )(table, before, *[half for block in blocks for half in block])


def body(embeddings, lengths):
    total = lax.axis_size("sample")
    here = lax.axis_index("sample")

    head, tail = make_unit(lengths, embeddings)
    my_h = shift(head, 1, 0)
    mz_h = shift(head, 0, 1)
    py_t = shift(tail, -1, 0)
    pz_t = shift(tail, 0, -1)
    sib_h = shift(head, 0, 0, 1)
    sib_t = shift(tail, 0, 0, 1)
    my_t = shift(tail, 1, 0)
    mz_t = shift(tail, 0, 1)
    py_h = shift(head, -1, 0)
    pz_h = shift(head, 0, -1)
    x_h = shift(my_h, 1, 0)
    y_h = shift(mz_h, 0, 1, flip=True)
    x_t = shift(py_t, -1, 0)
    y_t = shift(pz_t, 0, -1, flip=True)
    pyo_t = shift(py_t, 0, 0, 1)
    pzo_t = shift(pz_t, 0, 0, 1)
    pyo_h = shift(py_h, 0, 0, 1)
    pzo_h = shift(pz_h, 0, 0, 1)

    own = (head, tail)
    sib = (sib_h, sib_t)
    py, pyo, my = (py_h, py_t), (pyo_h, pyo_t), (my_h, my_t)
    pz, pzo, mz = (pz_h, pz_t), (pzo_h, pzo_t), (mz_h, mz_t)
    far_y, far_z = (x_h, x_t), (y_h, y_t)

    table = jnp.asarray(np.stack([plan(i) for i in range(total)]))[here]
    scores = jnp.zeros((total, 128), jnp.float32)
    scores = run_pairs(table, 0, 2, scores, [own, sib], "near_pairs")
    scores = run_pairs(
        table, 2, 10, scores, [own, sib, py, pyo, my, pz, pzo, mz], "mid_pairs"
    )
    scores = run_pairs(table, 12, 5, scores, [far_y, far_z, py, pyo, pz, pzo], "far_pairs")

    parts = lax.all_to_all(scores, "sample", 0, 0, tiled=True)
    mine = jnp.sum(parts, axis=0)
    ahead, behind = mine[:total], mine[total : 2 * total]
    offdiag = jnp.arange(total, dtype=jnp.int32) != here
    utility = jnp.sum(jnp.where(offdiag, ahead + behind, 0.0)) / jnp.float32(2 * (total - 1))
    return ahead[None, :], utility[None]


def solution(mesh):
    in_specs = (P(("prompt", "sample"), None, None), P(("prompt", "sample")))
    out_specs = (P(("prompt", "sample"), None), P(("prompt", "sample")))
    return jax.shard_map(body, mesh=mesh, in_specs=in_specs, out_specs=out_specs, check_vma=False)
```

```python
import functools

import jax
import jax.numpy as jnp
import numpy as np
from jax import lax
from jax.experimental import pallas as pl
from jax.experimental.pallas import tpu as pltpu
from jax.sharding import PartitionSpec as P

N = 4
HALF = 256
LEN = 2 * HALF
TAG = 16
VMEM = 24 * 2**20


def device(line, across, core):
    y, z = (across, line) if core == 0 else (line, across)
    return (y * N + z) * 2 + core


PLACES = [(line, across, core) for line in range(N) for across in range(N) for core in range(2)]


def near(i):
    return i ^ 1


def wide(i):
    return N - 1 - i


def along(x, step):
    moves = [(device(i, j, c), device(step(i), j, c)) for i, j, c in PLACES]
    return lax.ppermute(x, "sample", moves)


def over(x, step):
    moves = [(device(i, j, c), device(i, step(j), c)) for i, j, c in PLACES]
    return lax.ppermute(x, "sample", moves)


def swap(x):
    return lax.ppermute(x, "sample", [(i, i ^ 1) for i in range(2 * N * N)])


def unit_kernel(len_ref, emb_ref, full_ref, head_ref, tail_ref, raw, unit, sem):
    halves = (slice(0, HALF), slice(HALF, LEN))
    loads = [
        pltpu.make_async_copy(emb_ref.at[0, rows, :], raw.at[rows, :], sem.at[n])
        for n, rows in enumerate(halves)
    ]
    for load in loads:
        load.start()
    length = len_ref[0]
    lines = lax.broadcasted_iota(jnp.int32, (TAG, raw.shape[1]), 0)
    tag = jnp.where(lines < TAG // 2, length // 16, length % 16)
    unit[LEN : LEN + TAG, :] = tag.astype(jnp.float32).astype(jnp.bfloat16)
    stores = [
        pltpu.make_async_copy(
            unit.at[LEN : LEN + TAG, :], head_ref.at[HALF : HALF + TAG, :], sem.at[2]
        ),
        pltpu.make_async_copy(
            unit.at[LEN : LEN + TAG, :], full_ref.at[LEN : LEN + TAG, :], sem.at[3]
        ),
    ]
    for store in stores:
        store.start()
    first = None
    for n, rows in enumerate(halves):
        loads[n].wait()
        values = raw[rows, :].astype(jnp.float32)
        norm = jnp.sqrt(jnp.sum(values * values, axis=1, keepdims=True) + 1e-06)
        scaled = values / norm
        if first is None:
            first = scaled[0:1, :]
        places = lax.broadcasted_iota(jnp.int32, (HALF, 1), 0) + n * HALF
        unit[rows, :] = jnp.where(places < length, scaled, first).astype(jnp.bfloat16)
        part = head_ref.at[0:HALF, :] if n == 0 else tail_ref
        for k, target in enumerate((part, full_ref.at[rows, :])):
            store = pltpu.make_async_copy(unit.at[rows, :], target, sem.at[4 + 2 * n + k])
            store.start()
            stores.append(store)
    for store in stores:
        store.wait()


def make_unit(lengths, embeddings):
    width = embeddings.shape[2]
    rows = (LEN + TAG, HALF + TAG, HALF)
    return pl.pallas_call(
        unit_kernel,
        out_shape=tuple(jax.ShapeDtypeStruct((r, width), jnp.bfloat16) for r in rows),
        in_specs=[
            pl.BlockSpec(memory_space=pltpu.SMEM),
            pl.BlockSpec(memory_space=pltpu.HBM),
        ],
        out_specs=tuple(pl.BlockSpec(memory_space=pltpu.HBM) for _ in rows),
        scratch_shapes=[
            pltpu.VMEM((LEN, width), jnp.bfloat16),
            pltpu.VMEM((LEN + TAG, width), jnp.bfloat16),
            pltpu.SemaphoreType.DMA((8,)),
        ],
        compiler_params=pltpu.CompilerParams(vmem_limit_bytes=VMEM),
        name="unit",
    )(lengths, embeddings)


def plan(here):
    core = here % 2
    line, across = (here // 2 % N, here // 2 // N) if core == 0 else (here // 2 // N, here // 2 % N)
    low = across < N // 2

    def mine(i, j):
        return device(i, j, core)

    at = {
        "own": mine(line, across),
        "near": mine(near(line), across),
        "wide": mine(wide(line), across),
        "far": mine((line + 2) % N, across),
        "side": mine(line, wide(across)),
    }
    sender = near(across)
    at["next"] = mine(line, sender if sender in (0, N - 1) else wide(sender))
    for name, place in (
        ("sib", across),
        ("sib_near", near(across)),
        ("sib_wide", wide(across)),
        ("sib_far", (across + 2) % N),
    ):
        at[name] = device(place, line, 1 - core)

    early = [("own", "own")]
    if core == 0:
        early += [("own", "sib"), ("near", "sib")]
    else:
        early += [("near", "sib"), ("near", "sib_near")]
    if low:
        early += [("side", "own"), ("side", "near")]
    if line % 2 == 0:
        early += [("own", "near")]
    middle = [("wide", "sib"), ("wide", "sib_near")]
    if not low:
        middle += [("side", "wide")]
    if line % 2 == 1:
        middle += [("own", "wide")]
    if line in (1, 2):
        middle += [("near", "wide")]
    middle += [("next", "own"), ("next", "near"), ("next", "wide")]
    late = [("wide", "sib_wide")] if core == 1 else []
    late += [("far", "sib"), ("far", "sib_near"), ("far", "sib_wide"), ("next", "far")]
    if not low:
        late += [("side", "far")]
    if core == 0:
        late += [("far", "sib_far")]
    return at, (early, middle, late)


STAGES = (
    ("own", "near", "side", "sib", "sib_near"),
    ("own", "near", "wide", "side", "next", "sib", "sib_near"),
    ("far", "next", "side", "wide", "sib", "sib_near", "sib_wide", "sib_far"),
)


def make_table(total):
    plans = [plan(i) for i in range(total)]
    tables = []
    for stage, slots in enumerate(STAGES):
        steps = max((len(p[1][stage]) + 1) // 2 for p in plans)
        rows = np.zeros((total, 1 + 2 * steps, 8), np.int32)
        for i, (at, stages) in enumerate(plans):
            pairs = stages[stage]
            rows[i, 0, 0] = (len(pairs) + 1) // 2
            seen = set()
            for k, (u, v) in enumerate(pairs):
                waits = [0, 0]
                for n, s in enumerate((u, v)):
                    if s not in seen:
                        waits[n] = slots.index(s) + 1
                        seen.add(s)
                both = u != "own" or v != "own"
                rows[i, 1 + k] = (slots.index(u), slots.index(v), at[u], at[v], *waits, both, 0)
            if len(pairs) % 2:
                rows[i, 1 + len(pairs), :4] = (slots.index(u), slots.index(v), -1, -1)
            rest = [s for s in slots if s not in seen]
            rows[i, 0, 1] = sum(1 << slots.index(s) for s in rest)
        tables.append(rows.reshape(total, -1))
    starts = np.cumsum([0] + [t.shape[1] for t in tables])
    return np.concatenate(tables, axis=1), starts


def pairs_kernel(base, shapes, tab_ref, *refs):
    before_ref, refs = (None, refs) if base == 0 else (refs[0], refs[1:])
    ins = refs[: sum(shapes)]
    out_ref, tok, tag, sem = refs[sum(shapes) :]
    place = 0
    for s, parts in enumerate(shapes):
        head = ins[place]
        if parts == 1:
            tail, tags = head.at[HALF:LEN, :], head.at[LEN : LEN + TAG, 0:128]
        else:
            tail, tags = ins[place + 1], head.at[HALF : HALF + TAG, 0:128]
        place += parts
        pltpu.make_async_copy(head.at[0:HALF, :], tok.at[s, 0:HALF, :], sem.at[s, 0]).start()
        pltpu.make_async_copy(tail, tok.at[s, HALF:LEN, :], sem.at[s, 1]).start()
        pltpu.make_async_copy(tags, tag.at[s], sem.at[s, 2]).start()

    def arrive(s):
        for part in range(2):
            pltpu.make_async_copy(
                ins[0].at[0:HALF, :], tok.at[s, 0:HALF, :], sem.at[s, part]
            ).wait()
        pltpu.make_async_copy(ins[0].at[0:TAG, 0:128], tag.at[s], sem.at[s, 2]).wait()

    out_ref[...] = jnp.zeros_like(out_ref) if before_ref is None else before_ref[...]
    owners = lax.broadcasted_iota(jnp.int32, out_ref.shape, 0)
    lanes = lax.broadcasted_iota(jnp.int32, out_ref.shape, 1)
    total = out_ref.shape[0]
    rows = lax.broadcasted_iota(jnp.int32, (LEN, 1), 0).astype(jnp.float32)
    cols = lax.broadcasted_iota(jnp.int32, (1, LEN), 1).astype(jnp.float32)

    def length(s):
        value = tag[s].astype(jnp.float32)
        return value[0:1, 0:1] * 16.0 + value[TAG // 2 : TAG // 2 + 1, 0:1]

    def score(at):
        u, v = tab_ref[at], tab_ref[at + 1]
        own, other, both = tab_ref[at + 2], tab_ref[at + 3], tab_ref[at + 6]
        len_u, len_v = length(u), length(v)
        similar = lax.dot_general(
            tok[u], tok[v], (((1,), (1,)), ((), ())), preferred_element_type=jnp.float32
        )
        best_row = jnp.max(similar, axis=1, keepdims=True)
        best_col = jnp.max(similar, axis=0, keepdims=True)
        ahead = jnp.sum(jnp.where(rows < len_u, best_row, 0.0), axis=0, keepdims=True)
        behind = jnp.sum(jnp.where(cols < len_v, best_col, 0.0), axis=1, keepdims=True)
        ahead = ahead / len_u
        behind = behind / len_v
        at_u = owners == own
        at_v = (owners == other) & (both == 1)
        fore = (at_u & (lanes == other)) | (at_v & (lanes == total + own))
        back = (at_u & (lanes == total + other)) | (at_v & (lanes == own))
        return jnp.where(fore, ahead, 0.0) + jnp.where(back, behind, 0.0)

    @pl.loop(0, tab_ref[base])
    def _(step):
        first = base + 8 + 16 * step
        for wait in (4, 5, 12, 13):

            @pl.when(tab_ref[first + wait] > 0)
            def _():
                arrive(tab_ref[first + wait] - 1)

        out_ref[...] += score(first) + score(first + 8)

    rest = tab_ref[base + 1]
    for s in range(len(shapes)):

        @pl.when((rest >> s) % 2 == 1)
        def _():
            arrive(s)


def run_pairs(stage, table, starts, before, blocks):
    slots = [blocks[name] for name in STAGES[stage]]
    arrays = [half for block in slots for half in block]
    width = arrays[0].shape[1]
    before = [] if before is None else [before]
    steps = ((starts[stage + 1] - starts[stage]) // 8 - 1) // 2
    return pl.pallas_call(
        functools.partial(pairs_kernel, int(starts[stage]), [len(block) for block in slots]),
        out_shape=jax.ShapeDtypeStruct((2 * N * N, 128), jnp.float32),
        in_specs=[pl.BlockSpec(memory_space=pltpu.SMEM)]
        + [pl.BlockSpec(memory_space=pltpu.VMEM)] * len(before)
        + [pl.BlockSpec(memory_space=pltpu.HBM)] * len(arrays),
        out_specs=pl.BlockSpec(memory_space=pltpu.VMEM),
        scratch_shapes=[
            pltpu.VMEM((len(slots), LEN, width), jnp.bfloat16),
            pltpu.VMEM((len(slots), TAG, 128), jnp.bfloat16),
            pltpu.SemaphoreType.DMA((len(slots), 3)),
        ],
        compiler_params=pltpu.CompilerParams(vmem_limit_bytes=VMEM),
        cost_estimate=pl.CostEstimate(
            flops=int(4 * steps * LEN * LEN * width * 2),
            bytes_accessed=len(slots) * LEN * width * 2,
            transcendentals=0,
        ),
        name=f"pairs_{stage}",
    )(table, *before, *arrays)


def after(x, *others):
    return lax.optimization_barrier((x, *others))[0]


def body(embeddings, lengths):
    total = lax.axis_size("sample")
    here = lax.axis_index("sample")
    core, chip = here % 2, here // 2
    across = jnp.where(core == 0, chip // N, chip % N)
    edge = (across == 0) | (across == N - 1)

    full, head, tail = make_unit(lengths, embeddings)
    tables, starts = make_table(total)
    table = jnp.asarray(tables)[here]
    near_t = along(tail, near)
    side = over(full, wide)
    near_h = along(head, near)
    sib = swap(full)
    wide_h = along(after(head, side), wide)
    following = over(jnp.where(edge, full, side), near)
    wide_t = along(after(tail, side), wide)
    blocks = {
        "own": (full,),
        "near": (near_h, near_t),
        "side": (side,),
        "sib": (sib,),
        "sib_near": (swap(near_h), swap(near_t)),
    }
    scores = run_pairs(0, table, starts, None, blocks)
    far_h = along(after(wide_h, following, scores), near)
    far_t = along(after(near_t, wide_t, scores), wide)
    blocks |= {
        "wide": (wide_h, wide_t),
        "next": (following,),
    }
    scores = run_pairs(1, table, starts, scores, blocks)
    blocks |= {
        "far": (far_h, far_t),
        "sib_wide": (swap(wide_h), swap(wide_t)),
        "sib_far": (swap(after(far_h, scores)), swap(after(far_t, scores))),
    }
    scores = run_pairs(2, table, starts, scores, blocks)

    parts = lax.all_to_all(scores, "sample", 0, 0, tiled=True)
    result = jnp.sum(parts, axis=0)
    ahead, behind = result[:total], result[total : 2 * total]
    offdiag = jnp.arange(total, dtype=jnp.int32) != here
    utility = jnp.sum(jnp.where(offdiag, ahead + behind, 0.0)) / jnp.float32(2 * (total - 1))
    return ahead[None, :], utility[None]


def solution(mesh):
    in_specs = (P(("prompt", "sample"), None, None), P(("prompt", "sample")))
    out_specs = (P(("prompt", "sample"), None), P(("prompt", "sample")))
    return jax.shard_map(body, mesh=mesh, in_specs=in_specs, out_specs=out_specs, check_vma=False)
```

```python
import functools

import jax
import jax.numpy as jnp
import numpy as np
from jax import lax
from jax.experimental import pallas as pl
from jax.experimental.pallas import tpu as pltpu
from jax.sharding import PartitionSpec as P

N = 4
HALF = 256
LEN = 2 * HALF
TAG = 16
VMEM = 24 * 2**20


def device(line, across, core):
    y, z = (across, line) if core == 0 else (line, across)
    return (y * N + z) * 2 + core


PLACES = [(line, across, core) for line in range(N) for across in range(N) for core in range(2)]


def near(i):
    return i ^ 1


def wide(i):
    return N - 1 - i


def along(x, step):
    moves = [(device(i, j, c), device(step(i), j, c)) for i, j, c in PLACES]
    return lax.ppermute(x, "sample", moves)


def over(x, step):
    moves = [(device(i, j, c), device(i, step(j), c)) for i, j, c in PLACES]
    return lax.ppermute(x, "sample", moves)


def swap(x):
    return lax.ppermute(x, "sample", [(i, i ^ 1) for i in range(2 * N * N)])


def unit_kernel(len_ref, emb_ref, out_ref, unit, sem):
    length = len_ref[0]
    lines = lax.broadcasted_iota(jnp.int32, (TAG, unit.shape[1]), 0)
    tag = jnp.where(lines < TAG // 2, length // 16, length % 16)
    unit[LEN : LEN + TAG, :] = tag.astype(jnp.float32).astype(jnp.bfloat16)
    first, stores = None, []
    for n, end in enumerate((HALF, LEN + TAG)):
        start = n * HALF
        values = emb_ref[0, start : start + HALF, :].astype(jnp.float32)
        norm = jnp.sqrt(jnp.sum(values * values, axis=1, keepdims=True) + 1e-06)
        scaled = values / norm
        if first is None:
            first = scaled[0:1, :]
        places = lax.broadcasted_iota(jnp.int32, (HALF, 1), 0) + start
        unit[start : start + HALF, :] = jnp.where(places < length, scaled, first).astype(
            jnp.bfloat16
        )
        store = pltpu.make_async_copy(
            unit.at[start:end, :], out_ref.at[start:end, :], sem.at[n]
        )
        store.start()
        stores.append(store)
    for store in stores:
        store.wait()


def make_unit(lengths, embeddings):
    shape = (LEN + TAG, embeddings.shape[2])
    return pl.pallas_call(
        unit_kernel,
        out_shape=jax.ShapeDtypeStruct(shape, jnp.bfloat16),
        in_specs=[
            pl.BlockSpec(memory_space=pltpu.SMEM),
            pl.BlockSpec(memory_space=pltpu.VMEM),
        ],
        out_specs=pl.BlockSpec(memory_space=pltpu.HBM),
        scratch_shapes=[pltpu.VMEM(shape, jnp.bfloat16), pltpu.SemaphoreType.DMA((2,))],
        compiler_params=pltpu.CompilerParams(vmem_limit_bytes=VMEM),
        name="unit",
    )(lengths, embeddings)


def plan(here):
    core = here % 2
    line, across = (here // 2 % N, here // 2 // N) if core == 0 else (here // 2 // N, here // 2 % N)
    low = across < N // 2

    def mine(i, j):
        return device(i, j, core)

    at = {
        "own": mine(line, across),
        "near": mine(near(line), across),
        "wide": mine(wide(line), across),
        "far": mine((line + 2) % N, across),
        "side": mine(line, wide(across)),
    }
    sender = near(across)
    at["next"] = mine(line, sender if sender in (0, N - 1) else wide(sender))
    for name, place in (
        ("sib", across),
        ("sib_near", near(across)),
        ("sib_wide", wide(across)),
        ("sib_far", (across + 2) % N),
    ):
        at[name] = device(place, line, 1 - core)

    early = [("own", "own")]
    if core == 0:
        early += [("own", "sib"), ("near", "sib")]
    else:
        early += [("near", "sib"), ("near", "sib_near")]
    if line % 2 == 0:
        early += [("own", "near")]
    else:
        early += [("own", "wide")]
    if line in (1, 2):
        early += [("near", "wide")]
    early += [("wide", "sib"), ("wide", "sib_near")]
    if core == 1:
        early += [("wide", "sib_wide")]
    if low:
        middle = [("side", "own"), ("side", "near")]
    else:
        middle = [("side", "wide"), ("side", "far")]
    middle += [("far", "sib"), ("far", "sib_near"), ("far", "sib_wide")]
    if core == 0:
        middle += [("far", "sib_far")]
    late = [("next", "own"), ("next", "near"), ("next", "wide"), ("next", "far")]
    return at, (early, middle, late)


STAGES = (
    ("own", "sib", "near", "sib_near", "wide", "sib_wide"),
    ("side", "own", "near", "wide", "far", "sib", "sib_near", "sib_wide", "sib_far"),
    ("own", "next", "near", "wide", "far"),
)


def make_table(total):
    plans = [plan(i) for i in range(total)]
    tables = []
    for stage, slots in enumerate(STAGES):
        steps = max((len(p[1][stage]) + 1) // 2 for p in plans)
        rows = np.zeros((total, 1 + 2 * steps, 8), np.int32)
        for i, (at, stages) in enumerate(plans):
            pairs = stages[stage]
            rows[i, 0, 0] = (len(pairs) + 1) // 2
            seen = set()
            for k, (u, v) in enumerate(pairs):
                waits = [0, 0]
                for n, s in enumerate((u, v)):
                    if s not in seen:
                        waits[n] = slots.index(s) + 1
                        seen.add(s)
                both = u != "own" or v != "own"
                rows[i, 1 + k] = (slots.index(u), slots.index(v), at[u], at[v], *waits, both, 0)
            if len(pairs) % 2:
                rows[i, 1 + len(pairs), :4] = (slots.index(u), slots.index(v), -1, -1)
            rest = [s for s in slots if s not in seen]
            rows[i, 0, 1] = sum(1 << slots.index(s) for s in rest)
        tables.append(rows.reshape(total, -1))
    starts = np.cumsum([0] + [t.shape[1] for t in tables])
    return np.concatenate(tables, axis=1), starts


def pairs_kernel(base, slots, tab_ref, *refs):
    before_ref, refs = (None, refs) if base == 0 else (refs[0], refs[1:])
    ins = refs[:slots]
    out_ref, tok, tag, sem = refs[slots:]

    def copies(block, s):
        return (
            pltpu.make_async_copy(block.at[0:LEN, :], tok.at[s], sem.at[s, 0]),
            pltpu.make_async_copy(
                block.at[LEN : LEN + TAG, 0:128], tag.at[s], sem.at[s, 1]
            ),
        )

    for s in range(slots):
        for copy in copies(ins[s], s):
            copy.start()

    def arrive(s):
        for copy in copies(ins[0], s):
            copy.wait()

    out_ref[...] = jnp.zeros_like(out_ref) if before_ref is None else before_ref[...]
    owners = lax.broadcasted_iota(jnp.int32, out_ref.shape, 0)
    lanes = lax.broadcasted_iota(jnp.int32, out_ref.shape, 1)
    total = out_ref.shape[0]
    rows = lax.broadcasted_iota(jnp.int32, (LEN, 1), 0).astype(jnp.float32)
    cols = lax.broadcasted_iota(jnp.int32, (1, LEN), 1).astype(jnp.float32)

    def length(s):
        value = tag[s].astype(jnp.float32)
        return value[0:1, 0:1] * 16.0 + value[TAG // 2 : TAG // 2 + 1, 0:1]

    def score(at):
        u, v = tab_ref[at], tab_ref[at + 1]
        own, other, both = tab_ref[at + 2], tab_ref[at + 3], tab_ref[at + 6]
        len_u, len_v = length(u), length(v)
        similar = lax.dot_general(
            tok[u], tok[v], (((1,), (1,)), ((), ())), preferred_element_type=jnp.float32
        )
        best_row = jnp.max(similar, axis=1, keepdims=True)
        best_col = jnp.max(similar, axis=0, keepdims=True)
        ahead = jnp.sum(jnp.where(rows < len_u, best_row, 0.0), axis=0, keepdims=True)
        behind = jnp.sum(jnp.where(cols < len_v, best_col, 0.0), axis=1, keepdims=True)
        ahead = ahead / len_u
        behind = behind / len_v
        at_u = owners == own
        at_v = (owners == other) & (both == 1)
        fore = (at_u & (lanes == other)) | (at_v & (lanes == total + own))
        back = (at_u & (lanes == total + other)) | (at_v & (lanes == own))
        return jnp.where(fore, ahead, 0.0) + jnp.where(back, behind, 0.0)

    @pl.loop(0, tab_ref[base])
    def _(step):
        first = base + 8 + 16 * step
        for wait in (4, 5, 12, 13):

            @pl.when(tab_ref[first + wait] > 0)
            def _():
                arrive(tab_ref[first + wait] - 1)

        out_ref[...] += score(first) + score(first + 8)

    rest = tab_ref[base + 1]
    for s in range(slots):

        @pl.when((rest >> s) % 2 == 1)
        def _():
            arrive(s)


def run_pairs(stage, table, starts, before, blocks):
    arrays = [blocks[name] for name in STAGES[stage]]
    slots, width = len(arrays), arrays[0].shape[1]
    before = [] if before is None else [before]
    steps = ((starts[stage + 1] - starts[stage]) // 8 - 1) // 2
    return pl.pallas_call(
        functools.partial(pairs_kernel, int(starts[stage]), slots),
        out_shape=jax.ShapeDtypeStruct((2 * N * N, 128), jnp.float32),
        in_specs=[pl.BlockSpec(memory_space=pltpu.SMEM)]
        + [pl.BlockSpec(memory_space=pltpu.VMEM)] * len(before)
        + [pl.BlockSpec(memory_space=pltpu.HBM)] * slots,
        out_specs=pl.BlockSpec(memory_space=pltpu.VMEM),
        scratch_shapes=[
            pltpu.VMEM((slots, LEN, width), jnp.bfloat16),
            pltpu.VMEM((slots, TAG, 128), jnp.bfloat16),
            pltpu.SemaphoreType.DMA((slots, 2)),
        ],
        compiler_params=pltpu.CompilerParams(vmem_limit_bytes=VMEM),
        cost_estimate=pl.CostEstimate(
            flops=int(4 * steps * LEN * LEN * width * 2),
            bytes_accessed=slots * LEN * width * 2,
            transcendentals=0,
        ),
        name=f"pairs_{stage}",
    )(table, *before, *arrays)


def after(x, *others):
    return lax.optimization_barrier((x, *others))[0]


def body(embeddings, lengths):
    total = lax.axis_size("sample")
    here = lax.axis_index("sample")
    core, chip = here % 2, here // 2
    across = jnp.where(core == 0, chip // N, chip % N)
    edge = (across == 0) | (across == N - 1)

    tables, starts = make_table(total)
    table = jnp.asarray(tables)[here]
    blocks = {"own": make_unit(lengths, embeddings)}
    blocks["wide"] = along(blocks["own"], wide)
    blocks["near"] = along(blocks["own"], near)
    blocks["sib"] = swap(blocks["own"])
    blocks["side"] = over(after(blocks["own"], blocks["wide"]), wide)
    blocks["far"] = along(after(blocks["wide"], blocks["near"]), near)
    blocks["sib_near"] = swap(blocks["near"])
    blocks["sib_wide"] = swap(blocks["wide"])
    scores = run_pairs(0, table, starts, None, blocks)
    pick = jnp.where(edge, blocks["own"], after(blocks["side"], scores))
    blocks["next"] = over(after(pick, blocks["far"], scores), near)
    blocks["sib_far"] = swap(after(blocks["far"], scores))
    scores = run_pairs(1, table, starts, scores, blocks)
    scores = run_pairs(2, table, starts, scores, blocks)

    parts = lax.all_to_all(scores, "sample", 0, 0, tiled=True)
    result = jnp.sum(parts, axis=0)
    ahead, behind = result[:total], result[total : 2 * total]
    offdiag = jnp.arange(total, dtype=jnp.int32) != here
    utility = jnp.sum(jnp.where(offdiag, ahead + behind, 0.0)) / jnp.float32(2 * (total - 1))
    return ahead[None, :], utility[None]


def solution(mesh):
    in_specs = (P(("prompt", "sample"), None, None), P(("prompt", "sample")))
    out_specs = (P(("prompt", "sample"), None), P(("prompt", "sample")))
    return jax.shard_map(body, mesh=mesh, in_specs=in_specs, out_specs=out_specs, check_vma=False)
```

```python
import functools

import jax
import jax.numpy as jnp
import numpy as np
from jax import lax
from jax.experimental import pallas as pl
from jax.experimental.pallas import tpu as pltpu
from jax.sharding import PartitionSpec as P

N = 4
HALF = 256
LEN = 2 * HALF
TAG = 16
VMEM = 24 * 2**20


def device(line, across, core):
    y, z = (across, line) if core == 0 else (line, across)
    return (y * N + z) * 2 + core


PLACES = [(line, across, core) for line in range(N) for across in range(N) for core in range(2)]


def near(i):
    return i ^ 1


def wide(i):
    return N - 1 - i


def along(x, step):
    moves = [(device(i, j, c), device(step(i), j, c)) for i, j, c in PLACES]
    return lax.ppermute(x, "sample", moves)


def over(x, step):
    moves = [(device(i, j, c), device(i, step(j), c)) for i, j, c in PLACES]
    return lax.ppermute(x, "sample", moves)


def swap(x):
    return lax.ppermute(x, "sample", [(i, i ^ 1) for i in range(2 * N * N)])


def unit_kernel(len_ref, emb_ref, out_ref, unit, sem):
    length = len_ref[0]
    lines = lax.broadcasted_iota(jnp.int32, (TAG, unit.shape[1]), 0)
    tag = jnp.where(lines < TAG // 2, length // 16, length % 16)
    unit[LEN : LEN + TAG, :] = tag.astype(jnp.float32).astype(jnp.bfloat16)
    first, stores = None, []
    for n, end in enumerate((HALF, LEN + TAG)):
        start = n * HALF
        values = emb_ref[0, start : start + HALF, :].astype(jnp.float32)
        norm = jnp.sqrt(jnp.sum(values * values, axis=1, keepdims=True) + 1e-06)
        scaled = values / norm
        if first is None:
            first = scaled[0:1, :]
        places = lax.broadcasted_iota(jnp.int32, (HALF, 1), 0) + start
        unit[start : start + HALF, :] = jnp.where(places < length, scaled, first).astype(
            jnp.bfloat16
        )
        store = pltpu.make_async_copy(
            unit.at[start:end, :], out_ref.at[start:end, :], sem.at[n]
        )
        store.start()
        stores.append(store)
    for store in stores:
        store.wait()


def make_unit(lengths, embeddings):
    shape = (LEN + TAG, embeddings.shape[2])
    return pl.pallas_call(
        unit_kernel,
        out_shape=jax.ShapeDtypeStruct(shape, jnp.bfloat16),
        in_specs=[
            pl.BlockSpec(memory_space=pltpu.SMEM),
            pl.BlockSpec(memory_space=pltpu.VMEM),
        ],
        out_specs=pl.BlockSpec(memory_space=pltpu.HBM),
        scratch_shapes=[pltpu.VMEM(shape, jnp.bfloat16), pltpu.SemaphoreType.DMA((2,))],
        compiler_params=pltpu.CompilerParams(vmem_limit_bytes=VMEM),
        name="unit",
    )(lengths, embeddings)


def plan(here):
    core = here % 2
    line, across = (here // 2 % N, here // 2 // N) if core == 0 else (here // 2 // N, here // 2 % N)
    low = across < N // 2

    def mine(i, j):
        return device(i, j, core)

    at = {
        "own": mine(line, across),
        "near": mine(near(line), across),
        "wide": mine(wide(line), across),
        "far": mine((line + 2) % N, across),
        "side": mine(line, wide(across)),
    }
    sender = near(across)
    at["next"] = mine(line, sender if sender in (0, N - 1) else wide(sender))
    for name, place in (
        ("sib", across),
        ("sib_near", near(across)),
        ("sib_wide", wide(across)),
        ("sib_far", (across + 2) % N),
    ):
        at[name] = device(place, line, 1 - core)

    early = [("own", "own"), ("near", "sib"), ("wide", "sib")]
    if core == 0:
        early += [("own", "sib")]
    if line % 2 == 0:
        early += [("own", "near")]
    else:
        early += [("own", "wide")]
    if line in (1, 2):
        early += [("near", "wide")]
    if low:
        middle = [("side", "own"), ("side", "near")]
    else:
        middle = [("side", "wide"), ("side", "far")]
    middle += [("wide", "sib_near"), ("far", "sib"), ("far", "sib_near"), ("far", "sib_wide")]
    if core == 0:
        middle += [("far", "sib_far")]
    else:
        middle += [("near", "sib_near"), ("wide", "sib_wide")]
    late = [("next", "own"), ("next", "near"), ("next", "wide"), ("next", "far")]
    return at, (early, middle, late)


STAGES = (
    ("own", "near", "sib", "wide"),
    ("side", "own", "near", "wide", "far", "sib", "sib_near", "sib_wide", "sib_far"),
    ("next", "own", "near", "wide", "far"),
)


def make_table(total):
    plans = [plan(i) for i in range(total)]
    tables = []
    for stage, slots in enumerate(STAGES):
        steps = max((len(p[1][stage]) + 1) // 2 for p in plans)
        rows = np.zeros((total, 1 + 2 * steps, 8), np.int32)
        for i, (at, stages) in enumerate(plans):
            pairs = stages[stage]
            rows[i, 0, 0] = (len(pairs) + 1) // 2
            seen = set()
            for k, (u, v) in enumerate(pairs):
                waits = [0, 0]
                for n, s in enumerate((u, v)):
                    if s not in seen:
                        waits[n] = slots.index(s) + 1
                        seen.add(s)
                both = u != "own" or v != "own"
                rows[i, 1 + k] = (slots.index(u), slots.index(v), at[u], at[v], *waits, both, 0)
            if len(pairs) % 2:
                rows[i, 1 + len(pairs), :4] = (slots.index(u), slots.index(v), -1, -1)
            rest = [s for s in slots if s not in seen]
            rows[i, 0, 1] = sum(1 << slots.index(s) for s in rest)
        tables.append(rows.reshape(total, -1))
    starts = np.cumsum([0] + [t.shape[1] for t in tables])
    return np.concatenate(tables, axis=1), starts


def make_score(tab_ref, shape):
    owners = lax.broadcasted_iota(jnp.int32, shape, 0)
    lanes = lax.broadcasted_iota(jnp.int32, shape, 1)
    total = shape[0]
    rows = lax.broadcasted_iota(jnp.int32, (LEN, 1), 0).astype(jnp.float32)
    cols = lax.broadcasted_iota(jnp.int32, (1, LEN), 1).astype(jnp.float32)

    def length(tag):
        value = tag.astype(jnp.float32)
        return value[0:1, 0:1] * 16.0 + value[TAG // 2 : TAG // 2 + 1, 0:1]

    def score(at, tok_u, tok_v, tag_u, tag_v):
        own, other, both = tab_ref[at + 2], tab_ref[at + 3], tab_ref[at + 6]
        len_u, len_v = length(tag_u), length(tag_v)
        similar = lax.dot_general(
            tok_u, tok_v, (((1,), (1,)), ((), ())), preferred_element_type=jnp.float32
        )
        best_row = jnp.max(similar, axis=1, keepdims=True)
        best_col = jnp.max(similar, axis=0, keepdims=True)
        ahead = jnp.sum(jnp.where(rows < len_u, best_row, 0.0), axis=0, keepdims=True)
        behind = jnp.sum(jnp.where(cols < len_v, best_col, 0.0), axis=1, keepdims=True)
        ahead = ahead / len_u
        behind = behind / len_v
        at_u = owners == own
        at_v = (owners == other) & (both == 1)
        fore = (at_u & (lanes == other)) | (at_v & (lanes == total + own))
        back = (at_u & (lanes == total + other)) | (at_v & (lanes == own))
        return jnp.where(fore, ahead, 0.0) + jnp.where(back, behind, 0.0)

    return score


def last_kernel(base, tab_ref, before_ref, first_ref, *refs):
    *others, out_ref = refs
    score = make_score(tab_ref, out_ref.shape)
    result = before_ref[...]
    for k, block in enumerate(others):
        result += score(
            base + 8 + 8 * k,
            first_ref[0:LEN, :],
            block[0:LEN, :],
            first_ref[LEN : LEN + TAG, 0:128],
            block[LEN : LEN + TAG, 0:128],
        )
    out_ref[...] = result


def pairs_kernel(base, slots, tab_ref, *refs):
    before_ref, refs = (None, refs) if base == 0 else (refs[0], refs[1:])
    ins = refs[:slots]
    out_ref, tok, tag, sem = refs[slots:]

    def copies(block, s):
        return (
            pltpu.make_async_copy(block.at[0:LEN, :], tok.at[s], sem.at[s, 0]),
            pltpu.make_async_copy(
                block.at[LEN : LEN + TAG, 0:128], tag.at[s], sem.at[s, 1]
            ),
        )

    for s in range(slots):
        for copy in copies(ins[s], s):
            copy.start()

    def arrive(s):
        for copy in copies(ins[0], s):
            copy.wait()

    out_ref[...] = jnp.zeros_like(out_ref) if before_ref is None else before_ref[...]
    score_of = make_score(tab_ref, out_ref.shape)

    def score(at):
        u, v = tab_ref[at], tab_ref[at + 1]
        return score_of(at, tok[u], tok[v], tag[u], tag[v])

    @pl.loop(0, tab_ref[base])
    def _(step):
        first = base + 8 + 16 * step
        for wait in (4, 5, 12, 13):

            @pl.when(tab_ref[first + wait] > 0)
            def _():
                arrive(tab_ref[first + wait] - 1)

        out_ref[...] += score(first) + score(first + 8)

    rest = tab_ref[base + 1]
    for s in range(slots):

        @pl.when((rest >> s) % 2 == 1)
        def _():
            arrive(s)


def run_pairs(stage, table, starts, before, blocks):
    arrays = [blocks[name] for name in STAGES[stage]]
    slots, width = len(arrays), arrays[0].shape[1]
    before = [] if before is None else [before]
    steps = ((starts[stage + 1] - starts[stage]) // 8 - 1) // 2
    return pl.pallas_call(
        functools.partial(pairs_kernel, int(starts[stage]), slots),
        out_shape=jax.ShapeDtypeStruct((2 * N * N, 128), jnp.float32),
        in_specs=[pl.BlockSpec(memory_space=pltpu.SMEM)]
        + [pl.BlockSpec(memory_space=pltpu.VMEM)] * len(before)
        + [pl.BlockSpec(memory_space=pltpu.HBM)] * slots,
        out_specs=pl.BlockSpec(memory_space=pltpu.VMEM),
        scratch_shapes=[
            pltpu.VMEM((slots, LEN, width), jnp.bfloat16),
            pltpu.VMEM((slots, TAG, 128), jnp.bfloat16),
            pltpu.SemaphoreType.DMA((slots, 2)),
        ],
        compiler_params=pltpu.CompilerParams(vmem_limit_bytes=VMEM),
        cost_estimate=pl.CostEstimate(
            flops=int(4 * steps * LEN * LEN * width * 2) if stage < 2 else 0,
            bytes_accessed=slots * LEN * width * 2 if stage < 2 else 0,
            transcendentals=0,
        ),
        name=f"pairs_{stage}",
    )(table, *before, *arrays)


def run_last(stage, table, starts, before, blocks):
    arrays = [blocks[name] for name in STAGES[stage]]
    return pl.pallas_call(
        functools.partial(last_kernel, int(starts[stage])),
        out_shape=jax.ShapeDtypeStruct((2 * N * N, 128), jnp.float32),
        in_specs=[pl.BlockSpec(memory_space=pltpu.SMEM)]
        + [pl.BlockSpec(memory_space=pltpu.VMEM)] * (1 + len(arrays)),
        out_specs=pl.BlockSpec(memory_space=pltpu.VMEM),
        compiler_params=pltpu.CompilerParams(vmem_limit_bytes=VMEM),
        cost_estimate=pl.CostEstimate(flops=0, bytes_accessed=0, transcendentals=0),
        name=f"pairs_{stage}",
    )(table, before, *arrays)


def after(x, *others):
    return lax.optimization_barrier((x, *others))[0]


def body(embeddings, lengths):
    total = lax.axis_size("sample")
    here = lax.axis_index("sample")
    core, chip = here % 2, here // 2
    across = jnp.where(core == 0, chip // N, chip % N)
    edge = (across == 0) | (across == N - 1)

    tables, starts = make_table(total)
    table = jnp.asarray(tables)[here]
    blocks = {"own": make_unit(lengths, embeddings)}
    blocks["wide"] = along(blocks["own"], wide)
    blocks["near"] = along(blocks["own"], near)
    blocks["sib"] = swap(after(blocks["own"], table))
    blocks["side"] = over(after(blocks["own"], blocks["wide"]), wide)
    blocks["far"] = along(after(blocks["wide"], blocks["near"]), near)
    scores = run_pairs(0, table, starts, None, blocks)
    pick = jnp.where(edge, blocks["own"], after(blocks["side"], scores))
    blocks["next"] = over(pick, near)
    blocks["sib_near"] = swap(blocks["near"])
    blocks["sib_wide"] = swap(blocks["wide"])
    blocks["sib_far"] = swap(after(blocks["far"], pick))
    scores = run_pairs(1, table, starts, scores, blocks)
    scores = run_last(2, table, starts, scores, blocks)

    parts = lax.all_to_all(scores, "sample", 0, 0, tiled=True)
    result = jnp.sum(parts, axis=0)
    ahead, behind = result[:total], result[total : 2 * total]
    offdiag = jnp.arange(total, dtype=jnp.int32) != here
    utility = jnp.sum(jnp.where(offdiag, ahead + behind, 0.0)) / jnp.float32(2 * (total - 1))
    return ahead[None, :], utility[None]


def solution(mesh):
    in_specs = (P(("prompt", "sample"), None, None), P(("prompt", "sample")))
    out_specs = (P(("prompt", "sample"), None), P(("prompt", "sample")))
    return jax.shard_map(body, mesh=mesh, in_specs=in_specs, out_specs=out_specs, check_vma=False)
```

```python
import functools

import jax
import jax.numpy as jnp
import numpy as np
from jax import lax
from jax.experimental import pallas as pl
from jax.experimental.pallas import tpu as pltpu
from jax.sharding import PartitionSpec as P

N = 4
HALF = 256
LEN = 2 * HALF
TAG = 16
VMEM = 24 * 2**20


def device(line, across, core):
    y, z = (across, line) if core == 0 else (line, across)
    return (y * N + z) * 2 + core


PLACES = [(line, across, core) for line in range(N) for across in range(N) for core in range(2)]


def near(i):
    return i ^ 1


def wide(i):
    return N - 1 - i


def along(x, step):
    moves = [(device(i, j, c), device(step(i), j, c)) for i, j, c in PLACES]
    return lax.ppermute(x, "sample", moves)


def over(x, step):
    moves = [(device(i, j, c), device(i, step(j), c)) for i, j, c in PLACES]
    return lax.ppermute(x, "sample", moves)


def swap(x):
    return lax.ppermute(x, "sample", [(i, i ^ 1) for i in range(2 * N * N)])


def unit_kernel(len_ref, emb_ref, out_ref, unit, sem):
    length = len_ref[0]
    lines = lax.broadcasted_iota(jnp.int32, (TAG, unit.shape[1]), 0)
    tag = jnp.where(lines < TAG // 2, length // 16, length % 16)
    unit[LEN : LEN + TAG, :] = tag.astype(jnp.float32).astype(jnp.bfloat16)
    first, stores = None, []
    for n, end in enumerate((HALF, LEN + TAG)):
        start = n * HALF
        values = emb_ref[0, start : start + HALF, :].astype(jnp.float32)
        norm = jnp.sqrt(jnp.sum(values * values, axis=1, keepdims=True) + 1e-06)
        scaled = values / norm
        if first is None:
            first = scaled[0:1, :]
        places = lax.broadcasted_iota(jnp.int32, (HALF, 1), 0) + start
        unit[start : start + HALF, :] = jnp.where(places < length, scaled, first).astype(
            jnp.bfloat16
        )
        store = pltpu.make_async_copy(
            unit.at[start:end, :], out_ref.at[start:end, :], sem.at[n]
        )
        store.start()
        stores.append(store)
    for store in stores:
        store.wait()


def make_unit(lengths, embeddings):
    shape = (LEN + TAG, embeddings.shape[2])
    return pl.pallas_call(
        unit_kernel,
        out_shape=jax.ShapeDtypeStruct(shape, jnp.bfloat16),
        in_specs=[
            pl.BlockSpec(memory_space=pltpu.SMEM),
            pl.BlockSpec(memory_space=pltpu.VMEM),
        ],
        out_specs=pl.BlockSpec(memory_space=pltpu.HBM),
        scratch_shapes=[pltpu.VMEM(shape, jnp.bfloat16), pltpu.SemaphoreType.DMA((2,))],
        compiler_params=pltpu.CompilerParams(vmem_limit_bytes=VMEM),
        name="unit",
    )(lengths, embeddings)


NAMES = (
    "own",
    "near",
    "wide",
    "far",
    "side",
    "next",
    "sib",
    "sib_near",
    "sib_wide",
    "sib_far",
)
FLAGS = ("even", "odd", "inner", "low", "high", "first", "second")
STAGES = (
    (
        (None, (("near", "sib"), ("wide", "sib"))),
        ("even", (("own", "near"),)),
        ("odd", (("own", "wide"),)),
        ("inner", (("near", "wide"),)),
    ),
    (
        (None, (("far", "sib"), ("far", "sib_near"), ("wide", "sib_near"))),
        ("low", (("side", "own"), ("side", "near"))),
        ("high", (("side", "wide"), ("side", "far"))),
        ("second", (("near", "sib_near"),)),
    ),
    (
        (None, (("far", "sib_wide"),)),
        ("first", (("far", "sib_far"),)),
        ("second", (("wide", "sib_wide"),)),
    ),
    ((None, (("next", "own"), ("next", "near"), ("next", "wide"), ("next", "far"))),),
)


def plan(here):
    core = here % 2
    line, across = (here // 2 % N, here // 2 // N) if core == 0 else (here // 2 // N, here // 2 % N)
    sender = near(across)
    low = across < N // 2
    samples = (
        here,
        device(near(line), across, core),
        device(wide(line), across, core),
        device((line + 2) % N, across, core),
        device(line, wide(across), core),
        device(line, sender if sender in (0, N - 1) else wide(sender), core),
        device(across, line, 1 - core),
        device(near(across), line, 1 - core),
        device(wide(across), line, 1 - core),
        device((across + 2) % N, line, 1 - core),
    )
    flags = (line % 2 == 0, line % 2 == 1, line in (1, 2), low, not low, core == 0, core == 1)
    return np.array(samples + flags, np.int32)


def make_score(shape):
    owners = lax.broadcasted_iota(jnp.int32, shape, 0)
    lanes = lax.broadcasted_iota(jnp.int32, shape, 1)
    total = shape[0]
    rows = lax.broadcasted_iota(jnp.int32, (LEN, 1), 0).astype(jnp.float32)
    cols = lax.broadcasted_iota(jnp.int32, (1, LEN), 1).astype(jnp.float32)

    def length(tag):
        value = tag.astype(jnp.float32)
        return value[0:1, 0:1] * 16.0 + value[TAG // 2 : TAG // 2 + 1, 0:1]

    def score(own, other, both, tok_u, tok_v, tag_u, tag_v):
        len_u, len_v = length(tag_u), length(tag_v)
        similar = lax.dot_general(
            tok_u, tok_v, (((1,), (1,)), ((), ())), preferred_element_type=jnp.float32
        )
        best_row = jnp.max(similar, axis=1, keepdims=True)
        best_col = jnp.max(similar, axis=0, keepdims=True)
        ahead = jnp.sum(jnp.where(rows < len_u, best_row, 0.0), axis=0, keepdims=True)
        behind = jnp.sum(jnp.where(cols < len_v, best_col, 0.0), axis=1, keepdims=True)
        ahead = ahead / len_u
        behind = behind / len_v
        at_u = owners == own
        at_v = (owners == other) & (both == 1)
        fore = (at_u & (lanes == other)) | (at_v & (lanes == total + own))
        back = (at_u & (lanes == total + other)) | (at_v & (lanes == own))
        return jnp.where(fore, ahead, 0.0) + jnp.where(back, behind, 0.0)

    return score


def first_kernel(here_ref, own_ref, sib_ref, out_ref):
    score = make_score(out_ref.shape)
    here = here_ref[0]
    owner = jnp.where(here % 2 == 0, here, -1)
    own, own_tag = own_ref[0:LEN, :], own_ref[LEN : LEN + TAG, 0:128]
    out_ref[...] = score(here, here, 0, own, own, own_tag, own_tag) + score(
        owner, here + 1, 1 - here % 2, own, sib_ref[0:LEN, :], own_tag, sib_ref[LEN : LEN + TAG, 0:128]
    )


def run_first(here, own, sib):
    return pl.pallas_call(
        first_kernel,
        out_shape=jax.ShapeDtypeStruct((2 * N * N, 128), jnp.float32),
        in_specs=[pl.BlockSpec(memory_space=pltpu.SMEM)]
        + [pl.BlockSpec(memory_space=pltpu.VMEM)] * 2,
        out_specs=pl.BlockSpec(memory_space=pltpu.VMEM),
        compiler_params=pltpu.CompilerParams(vmem_limit_bytes=VMEM),
        cost_estimate=pl.CostEstimate(
            flops=4 * LEN * LEN * own.shape[1], bytes_accessed=2 * own.size, transcendentals=0
        ),
        name="pairs_0",
    )(here, own, sib)


def pairs_kernel(stage, names, parts, keep, tab_ref, before_ref, *refs):
    ins, out_ref = refs[: sum(parts)], refs[sum(parts)]
    score_of = make_score(out_ref.shape)
    blocks, place = {}, 0
    for name, count in zip(names, parts):
        blocks[name] = ins[place : place + count]
        place += count

    if keep:
        refs[-1][...] = blocks[keep][0][...]

    def tokens(name):
        *heads, last = blocks[name]
        rows = LEN - sum(head.shape[0] for head in heads)
        pieces = [head[...] for head in heads] + [last[0:rows, :]]
        pieces = pieces[0] if len(pieces) == 1 else jnp.concatenate(pieces, axis=0)
        return pieces, last[rows : rows + TAG, 0:128]

    def score(pairs):
        result = None
        for u, v in pairs:
            (tok_u, tag_u), (tok_v, tag_v) = tokens(u), tokens(v)
            own, other = tab_ref[NAMES.index(u)], tab_ref[NAMES.index(v)]
            part = score_of(own, other, 1, tok_u, tok_v, tag_u, tag_v)
            result = part if result is None else result + part
        return result

    result = before_ref[...]
    for flag, pairs in STAGES[stage]:
        if flag is None:
            out_ref[...] = result + score(pairs)
        else:

            @pl.when(tab_ref[len(NAMES) + FLAGS.index(flag)] == 1)
            def _():
                out_ref[...] += score(pairs)


def run_pairs(stage, table, before, blocks, keep=None):
    groups = [pair for _, pairs in STAGES[stage] for pair in pairs]
    names = sorted({name for pair in groups for name in pair} | ({keep} if keep else set()))
    chosen = [blocks[name] for name in names]
    chosen = [block if isinstance(block, tuple) else (block,) for block in chosen]
    arrays = [part for block in chosen for part in block]
    width = arrays[0].shape[1]
    hide = stage < 2
    outs = [jax.ShapeDtypeStruct(before.shape, jnp.float32)]
    outs += [jax.ShapeDtypeStruct(blocks[keep].shape, jnp.bfloat16)] if keep else []
    return pl.pallas_call(
        functools.partial(pairs_kernel, stage, names, [len(b) for b in chosen], keep),
        out_shape=outs,
        in_specs=[pl.BlockSpec(memory_space=pltpu.SMEM)]
        + [pl.BlockSpec(memory_space=pltpu.VMEM)] * (1 + len(arrays)),
        out_specs=[pl.BlockSpec(memory_space=pltpu.VMEM)] * len(outs),
        compiler_params=pltpu.CompilerParams(vmem_limit_bytes=VMEM),
        cost_estimate=pl.CostEstimate(
            flops=2 * len(groups) * LEN * LEN * width if hide else 0,
            bytes_accessed=len(names) * LEN * width * 2 if hide else 0,
            transcendentals=0,
        ),
        name=f"pairs_{stage + 1}",
    )(table, before, *arrays)


def after(x, *others):
    return lax.optimization_barrier((x, *others))[0]


def body(embeddings, lengths):
    total = lax.axis_size("sample")
    here = lax.axis_index("sample")
    core, chip = here % 2, here // 2
    across = jnp.where(core == 0, chip // N, chip % N)
    edge = (across == 0) | (across == N - 1)

    blocks = {"own": make_unit(lengths, embeddings)}
    table = jnp.asarray(np.stack([plan(i) for i in range(total)]))[here]
    blocks["wide"] = along(blocks["own"], wide)
    blocks["near"] = along(blocks["own"], near)
    blocks["sib"] = swap(after(blocks["own"], table))
    scores = run_first(here[None], blocks["own"], blocks["sib"])
    blocks["side"] = over(after(blocks["own"], blocks["wide"]), wide)
    blocks["far"] = along(after(blocks["wide"], blocks["near"]), near)
    blocks["sib_near"] = swap(blocks["near"])
    blocks["sib_wide"] = swap(blocks["wide"])
    (scores,) = run_pairs(0, table, scores, blocks)
    pick = jnp.where(edge, blocks["own"], after(blocks["side"], scores))
    blocks["next"] = over(pick, near)
    (scores,) = run_pairs(1, table, after(scores, pick), blocks)
    far = after(blocks["far"], scores)
    blocks["sib_far"] = (swap(far[:HALF]), swap(far[HALF:]))
    scores, blocks["near"] = run_pairs(2, table, scores, blocks, keep="near")
    (scores,) = run_pairs(3, table, scores, blocks)

    parts = lax.all_to_all(scores, "sample", 0, 0, tiled=True)
    result = jnp.sum(parts, axis=0)
    ahead, behind = result[:total], result[total : 2 * total]
    offdiag = jnp.arange(total, dtype=jnp.int32) != here
    utility = jnp.sum(jnp.where(offdiag, ahead + behind, 0.0)) / jnp.float32(2 * (total - 1))
    return ahead[None, :], utility[None]


def solution(mesh):
    in_specs = (P(("prompt", "sample"), None, None), P(("prompt", "sample")))
    out_specs = (P(("prompt", "sample"), None), P(("prompt", "sample")))
    return jax.shard_map(body, mesh=mesh, in_specs=in_specs, out_specs=out_specs, check_vma=False)
```

```python
import functools

import jax
import jax.numpy as jnp
import numpy as np
from jax import lax
from jax.experimental import pallas as pl
from jax.experimental.pallas import tpu as pltpu
from jax.sharding import PartitionSpec as P

N = 4
HALF = 256
LEN = 2 * HALF
TAG = 16
VMEM = 24 * 2**20


def device(line, across, core):
    y, z = (across, line) if core == 0 else (line, across)
    return (y * N + z) * 2 + core


PLACES = [(line, across, core) for line in range(N) for across in range(N) for core in range(2)]


def near(i):
    return i ^ 1


def wide(i):
    return N - 1 - i


def ahead_of(i):
    return (2, 0, 3, 1)[i]


def along(x, step):
    moves = [(device(i, j, c), device(step(i), j, c)) for i, j, c in PLACES]
    return lax.ppermute(x, "sample", moves)


def over(x, step):
    moves = [(device(i, j, c), device(i, step(j), c)) for i, j, c in PLACES]
    return lax.ppermute(x, "sample", moves)


def swap(x):
    return lax.ppermute(x, "sample", [(i, i ^ 1) for i in range(2 * N * N)])


def unit_kernel(len_ref, emb_ref, out_ref, unit, sem):
    length = len_ref[0]
    lines = lax.broadcasted_iota(jnp.int32, (TAG, unit.shape[1]), 0)
    tag = jnp.where(lines < TAG // 2, length // 16, length % 16)
    unit[LEN : LEN + TAG, :] = tag.astype(jnp.float32).astype(jnp.bfloat16)
    first, stores = None, []
    for n, end in enumerate((HALF, LEN + TAG)):
        start = n * HALF
        values = emb_ref[0, start : start + HALF, :].astype(jnp.float32)
        norm = jnp.sqrt(jnp.sum(values * values, axis=1, keepdims=True) + 1e-06)
        scaled = values / norm
        if first is None:
            first = scaled[0:1, :]
        places = lax.broadcasted_iota(jnp.int32, (HALF, 1), 0) + start
        unit[start : start + HALF, :] = jnp.where(places < length, scaled, first).astype(
            jnp.bfloat16
        )
        store = pltpu.make_async_copy(
            unit.at[start:end, :], out_ref.at[start:end, :], sem.at[n]
        )
        store.start()
        stores.append(store)
    for store in stores:
        store.wait()


def make_unit(lengths, embeddings):
    shape = (LEN + TAG, embeddings.shape[2])
    return pl.pallas_call(
        unit_kernel,
        out_shape=jax.ShapeDtypeStruct(shape, jnp.bfloat16),
        in_specs=[
            pl.BlockSpec(memory_space=pltpu.SMEM),
            pl.BlockSpec(memory_space=pltpu.VMEM),
        ],
        out_specs=pl.BlockSpec(memory_space=pltpu.HBM),
        scratch_shapes=[pltpu.VMEM(shape, jnp.bfloat16), pltpu.SemaphoreType.DMA((2,))],
        compiler_params=pltpu.CompilerParams(vmem_limit_bytes=VMEM),
        name="unit",
    )(lengths, embeddings)


NAMES = (
    "own",
    "near",
    "wide",
    "far",
    "side",
    "next",
    "sib",
    "sib_near",
    "sib_wide",
    "sib_far",
)
SIDE, NEXT, OTHER, ROWS = N, N + 1, 2 * N, 4 * N
FLAGS = ("even", "odd", "inner", "low", "high", "first", "second")
STAGES = (
    (
        (None, (("near", "sib"), ("wide", "sib"))),
        ("even", (("own", "near"),)),
        ("odd", (("own", "wide"),)),
        ("inner", (("near", "wide"),)),
    ),
    (
        (None, (("far", "sib"), ("far", "sib_near"), ("wide", "sib_near"))),
        ("low", (("side", "own"), ("side", "near"))),
        ("high", (("side", "wide"), ("side", "far"))),
        ("second", (("near", "sib_near"),)),
    ),
    (
        (None, (("far", "sib_wide"),)),
        ("first", (("far", "sib_far"),)),
        ("second", (("wide", "sib_wide"),)),
    ),
    ((None, (("next", "own"), ("next", "near"), ("next", "wide"), ("next", "far"))),),
)


def plan(here):
    core = here % 2
    line, across = (here // 2 % N, here // 2 // N) if core == 0 else (here // 2 // N, here // 2 % N)
    low = across < N // 2
    samples = (
        here,
        device(near(line), across, core),
        device(wide(line), across, core),
        device((line + 2) % N, across, core),
        device(line, wide(across), core),
        device(line, ahead_of(across), core),
        device(across, line, 1 - core),
        device(near(across), line, 1 - core),
        device(wide(across), line, 1 - core),
        device((across + 2) % N, line, 1 - core),
    )
    flags = (line % 2 == 0, line % 2 == 1, line in (1, 2), low, not low, core == 0, core == 1)
    lines = [(i, near(i), wide(i), (i + 2) % N) for i in (line, across)]
    rows = (*lines[0], SIDE, NEXT, *(OTHER + i for i in lines[1]))
    return np.array(samples + rows + flags, np.int32)


def make_score(shape, total=2 * N * N):
    owners = lax.broadcasted_iota(jnp.int32, shape, 0)
    lanes = lax.broadcasted_iota(jnp.int32, shape, 1)
    rows = lax.broadcasted_iota(jnp.int32, (LEN, 1), 0).astype(jnp.float32)
    cols = lax.broadcasted_iota(jnp.int32, (1, LEN), 1).astype(jnp.float32)

    def length(tag):
        value = tag.astype(jnp.float32)
        return value[0:1, 0:1] * 16.0 + value[TAG // 2 : TAG // 2 + 1, 0:1]

    def score(row_u, row_v, own, other, both, tok_u, tok_v, tag_u, tag_v):
        len_u, len_v = length(tag_u), length(tag_v)
        similar = lax.dot_general(
            tok_u, tok_v, (((1,), (1,)), ((), ())), preferred_element_type=jnp.float32
        )
        best_row = jnp.max(similar, axis=1, keepdims=True)
        best_col = jnp.max(similar, axis=0, keepdims=True)
        ahead = jnp.sum(jnp.where(rows < len_u, best_row, 0.0), axis=0, keepdims=True)
        behind = jnp.sum(jnp.where(cols < len_v, best_col, 0.0), axis=1, keepdims=True)
        ahead = ahead / len_u
        behind = behind / len_v
        at_u = owners == row_u
        at_v = (owners == row_v) & (both == 1)
        fore = (at_u & (lanes == other)) | (at_v & (lanes == total + own))
        back = (at_u & (lanes == total + other)) | (at_v & (lanes == own))
        return jnp.where(fore, ahead, 0.0) + jnp.where(back, behind, 0.0)

    return score


def first_kernel(here_ref, own_ref, sib_ref, out_ref):
    score = make_score(out_ref.shape)
    here = here_ref[0]
    first, y, z = 1 - here % 2, here // 2 // N, here // 2 % N
    line = jnp.where(first == 1, z, y)
    own, own_tag = own_ref[0:LEN, :], own_ref[LEN : LEN + TAG, 0:128]
    sib, sib_tag = sib_ref[0:LEN, :], sib_ref[LEN : LEN + TAG, 0:128]
    row = jnp.where(first == 1, line, -1)
    out_ref[...] = score(line, line, here, here, 0, own, own, own_tag, own_tag) + score(
        row, OTHER + y, here, here + 1, first, own, sib, own_tag, sib_tag
    )


def run_first(here, own, sib):
    return pl.pallas_call(
        first_kernel,
        out_shape=jax.ShapeDtypeStruct((ROWS, 128), jnp.float32),
        in_specs=[pl.BlockSpec(memory_space=pltpu.SMEM)]
        + [pl.BlockSpec(memory_space=pltpu.VMEM)] * 2,
        out_specs=pl.BlockSpec(memory_space=pltpu.VMEM),
        compiler_params=pltpu.CompilerParams(vmem_limit_bytes=VMEM),
        cost_estimate=pl.CostEstimate(
            flops=4 * LEN * LEN * own.shape[1], bytes_accessed=2 * own.size, transcendentals=0
        ),
        name="pairs_0",
    )(here, own, sib)


def pairs_kernel(stage, names, parts, keep, tab_ref, before_ref, *refs):
    last = stage == len(STAGES) - 1
    given_ref, refs = (refs[0], refs[1:]) if last else (None, refs)
    ins, out_ref = refs[: sum(parts)], refs[sum(parts)]
    score_of = make_score(before_ref.shape)
    blocks, place = {}, 0
    for name, count in zip(names, parts):
        blocks[name] = ins[place : place + count]
        place += count

    if keep:
        refs[-1][...] = blocks[keep][0][...]

    def tokens(name):
        *heads, last = blocks[name]
        rows = LEN - sum(head.shape[0] for head in heads)
        pieces = [head[...] for head in heads] + [last[0:rows, :]]
        pieces = pieces[0] if len(pieces) == 1 else jnp.concatenate(pieces, axis=0)
        return pieces, last[rows : rows + TAG, 0:128]

    def score(pairs):
        result = None
        for u, v in pairs:
            (tok_u, tag_u), (tok_v, tag_v) = tokens(u), tokens(v)
            at, to = NAMES.index(u), NAMES.index(v)
            row_u, row_v = tab_ref[len(NAMES) + at], tab_ref[len(NAMES) + to]
            part = score_of(row_u, row_v, tab_ref[at], tab_ref[to], 1, tok_u, tok_v, tag_u, tag_v)
            result = part if result is None else result + part
        return result

    result = before_ref[...]
    for flag, pairs in STAGES[stage]:
        if last:
            result += score(pairs)
            out_ref[...] = result[0:N] + given_ref[OTHER : OTHER + N, :]
            refs[-1][...] = jnp.broadcast_to(result[NEXT : NEXT + 1], refs[-1].shape)
        elif flag is None:
            out_ref[...] = result + score(pairs)
        else:

            @pl.when(tab_ref[2 * len(NAMES) + FLAGS.index(flag)] == 1)
            def _():
                out_ref[...] += score(pairs)


def run_pairs(stage, table, before, blocks, keep=None, given=()):
    groups = [pair for _, pairs in STAGES[stage] for pair in pairs]
    names = sorted({name for pair in groups for name in pair} | ({keep} if keep else set()))
    chosen = [blocks[name] for name in names]
    chosen = [block if isinstance(block, tuple) else (block,) for block in chosen]
    arrays = [part for block in chosen for part in block]
    width = arrays[0].shape[1]
    hide = stage < 2
    shapes = [(N, 128), (2 * N, 128)] if given else [before.shape]
    outs = [jax.ShapeDtypeStruct(shape, jnp.float32) for shape in shapes]
    outs += [jax.ShapeDtypeStruct(blocks[keep].shape, jnp.bfloat16)] if keep else []
    return pl.pallas_call(
        functools.partial(pairs_kernel, stage, names, [len(b) for b in chosen], keep),
        out_shape=outs,
        in_specs=[pl.BlockSpec(memory_space=pltpu.SMEM)]
        + [pl.BlockSpec(memory_space=pltpu.VMEM)] * (1 + len(given) + len(arrays)),
        out_specs=[pl.BlockSpec(memory_space=pltpu.VMEM)] * len(outs),
        compiler_params=pltpu.CompilerParams(vmem_limit_bytes=VMEM),
        cost_estimate=pl.CostEstimate(
            flops=2 * len(groups) * LEN * LEN * width if hide else 0,
            bytes_accessed=len(names) * LEN * width * 2 if hide else 0,
            transcendentals=0,
        ),
        name=f"pairs_{stage + 1}",
    )(table, before, *given, *arrays)


def after(x, *others):
    return lax.optimization_barrier((x, *others))[0]


def body(embeddings, lengths):
    total = lax.axis_size("sample")
    here = lax.axis_index("sample")
    core, chip = here % 2, here // 2
    across = jnp.where(core == 0, chip // N, chip % N)
    edge = (across == 0) | (across == N - 1)

    blocks = {"own": make_unit(lengths, embeddings)}
    table = jnp.asarray(np.stack([plan(i) for i in range(total)]))[here]
    blocks["wide"] = along(blocks["own"], wide)
    blocks["near"] = along(blocks["own"], near)
    blocks["sib"] = swap(after(blocks["own"], table))
    scores = run_first(here[None], blocks["own"], blocks["sib"])
    blocks["side"] = over(after(blocks["own"], blocks["wide"]), wide)
    blocks["far"] = along(after(blocks["wide"], blocks["near"]), near)
    blocks["sib_near"] = swap(blocks["near"])
    blocks["sib_wide"] = swap(blocks["wide"])
    (scores,) = run_pairs(0, table, scores, blocks)
    pick = jnp.where(edge, blocks["own"], after(blocks["side"], scores))
    blocks["next"] = over(pick, near)
    (scores,) = run_pairs(1, table, after(scores, pick), blocks)
    from_side = over(scores, wide)
    far = after(blocks["far"], scores)
    blocks["sib_far"] = (swap(far[:HALF]), swap(far[HALF:]))
    scores, blocks["near"] = run_pairs(2, table, scores, blocks, keep="near")
    line, last = run_pairs(3, table, scores, blocks, given=(swap(scores),))

    from_next = over(last, ahead_of)
    groups = [[device(i, j, c) for i in range(N)] for j in range(N) for c in range(2)]
    parts = lax.all_to_all(line, "sample", 0, 0, tiled=True, axis_index_groups=groups)
    result = jnp.sum(parts, axis=0) + from_side[SIDE] + from_next[0]
    ahead, behind = result[:total], result[total : 2 * total]
    offdiag = jnp.arange(total, dtype=jnp.int32) != here
    utility = jnp.sum(jnp.where(offdiag, ahead + behind, 0.0)) / jnp.float32(2 * (total - 1))
    return ahead[None, :], utility[None]


def solution(mesh):
    in_specs = (P(("prompt", "sample"), None, None), P(("prompt", "sample")))
    out_specs = (P(("prompt", "sample"), None), P(("prompt", "sample")))
    return jax.shard_map(body, mesh=mesh, in_specs=in_specs, out_specs=out_specs, check_vma=False)
```

```python
import functools

import jax
import jax.numpy as jnp
import numpy as np
from jax import lax
from jax.experimental import pallas as pl
from jax.experimental.pallas import tpu as pltpu
from jax.sharding import PartitionSpec as P

N = 4
HALF = 256
LEN = 2 * HALF
TAG = 16
VMEM = 24 * 2**20


def device(line, across, core):
    y, z = (across, line) if core == 0 else (line, across)
    return (y * N + z) * 2 + core


PLACES = [(line, across, core) for line in range(N) for across in range(N) for core in range(2)]


def near(i):
    return i ^ 1


def wide(i):
    return N - 1 - i


def across_from(i):
    return (i + 2) % N


def ahead_of(i):
    return (2, 0, 3, 1)[i]


def along(x, step):
    moves = [(device(i, j, c), device(step(i), j, c)) for i, j, c in PLACES]
    return lax.ppermute(x, "sample", moves)


def over(x, step):
    moves = [(device(i, j, c), device(i, step(j), c)) for i, j, c in PLACES]
    return lax.ppermute(x, "sample", moves)


def swap(x):
    return lax.ppermute(x, "sample", [(i, i ^ 1) for i in range(2 * N * N)])


def unit_kernel(len_ref, emb_ref, out_ref, unit, sem):
    length = len_ref[0]
    lines = lax.broadcasted_iota(jnp.int32, (TAG, unit.shape[1]), 0)
    tag = jnp.where(lines < TAG // 2, length // 16, length % 16)
    unit[LEN : LEN + TAG, :] = tag.astype(jnp.float32).astype(jnp.bfloat16)
    first, stores = None, []
    for n, end in enumerate((HALF, LEN + TAG)):
        start = n * HALF
        values = emb_ref[0, start : start + HALF, :].astype(jnp.float32)
        norm = jnp.sqrt(jnp.sum(values * values, axis=1, keepdims=True) + 1e-06)
        scaled = values / norm
        if first is None:
            first = scaled[0:1, :]
        places = lax.broadcasted_iota(jnp.int32, (HALF, 1), 0) + start
        unit[start : start + HALF, :] = jnp.where(places < length, scaled, first).astype(
            jnp.bfloat16
        )
        store = pltpu.make_async_copy(
            unit.at[start:end, :], out_ref.at[start:end, :], sem.at[n]
        )
        store.start()
        stores.append(store)
    for store in stores:
        store.wait()


def make_unit(lengths, embeddings):
    shape = (LEN + TAG, embeddings.shape[2])
    return pl.pallas_call(
        unit_kernel,
        out_shape=jax.ShapeDtypeStruct(shape, jnp.bfloat16),
        in_specs=[
            pl.BlockSpec(memory_space=pltpu.SMEM),
            pl.BlockSpec(memory_space=pltpu.VMEM),
        ],
        out_specs=pl.BlockSpec(memory_space=pltpu.HBM),
        scratch_shapes=[pltpu.VMEM(shape, jnp.bfloat16), pltpu.SemaphoreType.DMA((2,))],
        compiler_params=pltpu.CompilerParams(vmem_limit_bytes=VMEM),
        name="unit",
    )(lengths, embeddings)


NAMES = (
    "own",
    "near",
    "wide",
    "far",
    "side",
    "next",
    "sib",
    "sib_near",
    "sib_wide",
    "sib_far",
)
SIDE, NEXT, OTHER, ROWS = N, N + 1, 2 * N, 4 * N
FLAGS = ("even", "odd", "inner", "low", "high", "first", "second", "edge")
STAGES = (
    (
        (None, (("near", "sib"), ("wide", "sib"))),
        ("even", (("own", "near"),)),
        ("odd", (("own", "wide"),)),
        ("inner", (("near", "wide"),)),
    ),
    (
        (None, (("far", "sib"), ("far", "sib_near"), ("wide", "sib_near"))),
        ("low", (("side", "own"), ("side", "near"))),
        ("high", (("side", "wide"), ("side", "far"))),
        ("second", (("near", "sib_near"),)),
    ),
    (
        (None, (("far", "sib_wide"),)),
        ("first", (("far", "sib_far"),)),
        ("second", (("wide", "sib_wide"),)),
    ),
    ((None, (("next", "own"), ("next", "near"), ("next", "wide"), ("next", "far"))),),
)


def plan(here):
    core = here % 2
    line, across = (here // 2 % N, here // 2 // N) if core == 0 else (here // 2 // N, here // 2 % N)
    low = across < N // 2
    samples = (
        here,
        device(near(line), across, core),
        device(wide(line), across, core),
        device((line + 2) % N, across, core),
        device(line, wide(across), core),
        device(line, ahead_of(across), core),
        device(across, line, 1 - core),
        device(near(across), line, 1 - core),
        device(wide(across), line, 1 - core),
        device((across + 2) % N, line, 1 - core),
    )
    flags = (line % 2 == 0, line % 2 == 1, line in (1, 2), low, not low, core == 0, core == 1)
    flags += (across in (0, N - 1),)
    rows = (*range(N), SIDE, NEXT, *range(OTHER, OTHER + N))
    return np.array(samples + rows + flags, np.int32)


def make_score(shape, total=2 * N * N):
    owners = lax.broadcasted_iota(jnp.int32, shape, 0)
    lanes = lax.broadcasted_iota(jnp.int32, shape, 1)
    rows = lax.broadcasted_iota(jnp.int32, (LEN, 1), 0).astype(jnp.float32)
    cols = lax.broadcasted_iota(jnp.int32, (1, LEN), 1).astype(jnp.float32)

    def length(tag):
        value = tag.astype(jnp.float32)
        return value[0:1, 0:1] * 16.0 + value[TAG // 2 : TAG // 2 + 1, 0:1]

    def score(row_u, row_v, own, other, both, tok_u, tok_v, tag_u, tag_v):
        len_u, len_v = length(tag_u), length(tag_v)
        similar = lax.dot_general(
            tok_u, tok_v, (((1,), (1,)), ((), ())), preferred_element_type=jnp.float32
        )
        best_row = jnp.max(similar, axis=1, keepdims=True)
        best_col = jnp.max(similar, axis=0, keepdims=True)
        ahead = jnp.sum(jnp.where(rows < len_u, best_row, 0.0), axis=0, keepdims=True)
        behind = jnp.sum(jnp.where(cols < len_v, best_col, 0.0), axis=1, keepdims=True)
        ahead = ahead / len_u
        behind = behind / len_v
        at_u = owners == row_u
        at_v = (owners == row_v) & (both == 1)
        fore = (at_u & (lanes == other)) | (at_v & (lanes == total + own))
        back = (at_u & (lanes == total + other)) | (at_v & (lanes == own))
        return jnp.where(fore, ahead, 0.0) + jnp.where(back, behind, 0.0)

    return score


def first_kernel(here_ref, own_ref, sib_ref, out_ref):
    score = make_score(out_ref.shape)
    here = here_ref[0]
    first = 1 - here % 2
    own, own_tag = own_ref[0:LEN, :], own_ref[LEN : LEN + TAG, 0:128]
    sib, sib_tag = sib_ref[0:LEN, :], sib_ref[LEN : LEN + TAG, 0:128]
    row = jnp.where(first == 1, 0, -1)
    out_ref[...] = score(0, 0, here, here, 0, own, own, own_tag, own_tag) + score(
        row, OTHER, here, here + 1, first, own, sib, own_tag, sib_tag
    )


def run_first(here, own, sib):
    return pl.pallas_call(
        first_kernel,
        out_shape=jax.ShapeDtypeStruct((ROWS, 128), jnp.float32),
        in_specs=[pl.BlockSpec(memory_space=pltpu.SMEM)]
        + [pl.BlockSpec(memory_space=pltpu.VMEM)] * 2,
        out_specs=pl.BlockSpec(memory_space=pltpu.VMEM),
        compiler_params=pltpu.CompilerParams(vmem_limit_bytes=VMEM),
        cost_estimate=pl.CostEstimate(
            flops=4 * LEN * LEN * own.shape[1], bytes_accessed=2 * own.size, transcendentals=0
        ),
        name="pairs_0",
    )(here, own, sib)


def pairs_kernel(stage, names, parts, keep, tab_ref, before_ref, *refs):
    last = stage == len(STAGES) - 1
    given_ref, refs = (refs[0], refs[1:]) if last else (None, refs)
    ins, out_ref = refs[: sum(parts)], refs[sum(parts)]
    score_of = make_score(before_ref.shape)
    blocks, place = {}, 0
    for name, count in zip(names, parts):
        blocks[name] = ins[place : place + count]
        place += count

    if keep:
        refs[-1][...] = blocks[keep][0][...]

    def tokens(name):
        *heads, last = blocks[name]
        rows = LEN - sum(head.shape[0] for head in heads)
        pieces = [head[...] for head in heads] + [last[0:rows, :]]
        pieces = pieces[0] if len(pieces) == 1 else jnp.concatenate(pieces, axis=0)
        return pieces, last[rows : rows + TAG, 0:128]

    def score(pairs):
        result = None
        for u, v in pairs:
            (tok_u, tag_u), (tok_v, tag_v) = tokens(u), tokens(v)
            at, to = NAMES.index(u), NAMES.index(v)
            row_u, row_v = tab_ref[len(NAMES) + at], tab_ref[len(NAMES) + to]
            part = score_of(row_u, row_v, tab_ref[at], tab_ref[to], 1, tok_u, tok_v, tag_u, tag_v)
            result = part if result is None else result + part
        return result

    result = before_ref[...]
    for flag, pairs in STAGES[stage]:
        if last:
            result += score(pairs)
            line = result[0:N] + given_ref[OTHER : OTHER + N, :]
            for k, ref in enumerate(refs[sum(parts) :]):
                row = line[k : k + 1] if k < N else result[NEXT : NEXT + 1]
                ref[...] = jnp.broadcast_to(row, ref.shape)
        elif flag is None:
            out_ref[...] = result + score(pairs)
        else:

            @pl.when(tab_ref[2 * len(NAMES) + FLAGS.index(flag)] == 1)
            def _():
                out_ref[...] += score(pairs)


def run_pairs(stage, table, before, blocks, keep=None, given=()):
    groups = [pair for _, pairs in STAGES[stage] for pair in pairs]
    names = sorted({name for pair in groups for name in pair} | ({keep} if keep else set()))
    chosen = [blocks[name] for name in names]
    chosen = [block if isinstance(block, tuple) else (block,) for block in chosen]
    arrays = [part for block in chosen for part in block]
    width = arrays[0].shape[1]
    hide = stage < 2
    shapes = [(2 * N, 128)] * (N + 1) if given else [before.shape]
    outs = [jax.ShapeDtypeStruct(shape, jnp.float32) for shape in shapes]
    outs += [jax.ShapeDtypeStruct(blocks[keep].shape, jnp.bfloat16)] if keep else []
    return pl.pallas_call(
        functools.partial(pairs_kernel, stage, names, [len(b) for b in chosen], keep),
        out_shape=outs,
        in_specs=[pl.BlockSpec(memory_space=pltpu.SMEM)]
        + [pl.BlockSpec(memory_space=pltpu.VMEM)] * (1 + len(given) + len(arrays)),
        out_specs=[pl.BlockSpec(memory_space=pltpu.VMEM)] * len(outs),
        compiler_params=pltpu.CompilerParams(vmem_limit_bytes=VMEM),
        cost_estimate=pl.CostEstimate(
            flops=2 * len(groups) * LEN * LEN * width if hide else 0,
            bytes_accessed=len(names) * LEN * width * 2 if hide else 0,
            transcendentals=0,
        ),
        name=f"pairs_{stage + 1}",
    )(table, before, *given, *arrays)


def pick_kernel(tab_ref, own_ref, side_ref, out_ref, sem):
    edge = tab_ref[2 * len(NAMES) + FLAGS.index("edge")]
    step = (LEN + TAG) // 3
    for flag, block in ((1, own_ref), (0, side_ref)):

        @pl.when(edge == flag)
        def _():
            copies = []
            for k in range(3):
                rows = pl.ds(k * step, step)
                copies.append(
                    pltpu.make_async_copy(block.at[rows, :], out_ref.at[rows, :], sem.at[k])
                )
            for copy in copies:
                copy.start()
            for copy in copies:
                copy.wait()


def run_pick(table, own, side):
    return pl.pallas_call(
        pick_kernel,
        out_shape=jax.ShapeDtypeStruct(own.shape, own.dtype),
        in_specs=[pl.BlockSpec(memory_space=pltpu.SMEM)]
        + [pl.BlockSpec(memory_space=pl.ANY)] * 2,
        out_specs=pl.BlockSpec(memory_space=pl.ANY),
        scratch_shapes=[pltpu.SemaphoreType.DMA((3,))],
        compiler_params=pltpu.CompilerParams(vmem_limit_bytes=VMEM),
        cost_estimate=pl.CostEstimate(flops=0, bytes_accessed=0, transcendentals=0),
        name="pick",
    )(table, own, side)


def after(x, *others):
    return lax.optimization_barrier((x, *others))[0]


def body(embeddings, lengths):
    total = lax.axis_size("sample")
    here = lax.axis_index("sample")
    blocks = {"own": make_unit(lengths, embeddings)}
    table = jnp.asarray(np.stack([plan(i) for i in range(total)]))[here]
    blocks["wide"] = along(blocks["own"], wide)
    blocks["near"] = along(blocks["own"], near)
    blocks["sib"] = swap(after(blocks["own"], table))
    scores = run_first(here[None], blocks["own"], blocks["sib"])
    blocks["side"] = over(after(blocks["own"], blocks["wide"]), wide)
    blocks["far"] = along(after(blocks["wide"], blocks["near"]), near)
    blocks["sib_near"] = swap(blocks["near"])
    blocks["sib_wide"] = swap(blocks["wide"])
    (scores,) = run_pairs(0, table, scores, blocks)
    pick = run_pick(table, blocks["own"], after(blocks["side"], scores))
    blocks["next"] = over(pick, near)
    (scores,) = run_pairs(1, table, after(scores, pick), blocks)
    from_side = over(scores, wide)
    far = after(blocks["far"], scores)
    blocks["sib_far"] = (swap(far[:HALF]), swap(far[HALF:]))
    scores, blocks["near"] = run_pairs(2, table, scores, blocks, keep="near")
    mine, *rest = run_pairs(3, table, scores, blocks, given=(swap(scores),))
    result = mine[0] + from_side[SIDE]
    for rows, step in zip(rest, (near, wide, across_from)):
        result += along(rows, step)[0]
    result += over(rest[-1], ahead_of)[0]
    ahead, behind = result[:total], result[total : 2 * total]
    offdiag = jnp.arange(total, dtype=jnp.int32) != here
    utility = jnp.sum(jnp.where(offdiag, ahead + behind, 0.0)) / jnp.float32(2 * (total - 1))
    return ahead[None, :], utility[None]


def solution(mesh):
    in_specs = (P(("prompt", "sample"), None, None), P(("prompt", "sample")))
    out_specs = (P(("prompt", "sample"), None), P(("prompt", "sample")))
    return jax.shard_map(body, mesh=mesh, in_specs=in_specs, out_specs=out_specs, check_vma=False)
```

```python
import functools

import jax
import jax.numpy as jnp
import numpy as np
from jax import lax
from jax.experimental import pallas as pl
from jax.experimental.pallas import tpu as pltpu
from jax.sharding import PartitionSpec as P

N = 4
HALF = 256
LEN = 2 * HALF
TAG = 16
VMEM = 24 * 2**20


def device(line, across, core):
    y, z = (across, line) if core == 0 else (line, across)
    return (y * N + z) * 2 + core


PLACES = [(line, across, core) for line in range(N) for across in range(N) for core in range(2)]


def near(i):
    return i ^ 1


def wide(i):
    return N - 1 - i


def across_from(i):
    return (i + 2) % N


def ahead_of(i):
    return (2, 0, 3, 1)[i]


def along(x, step):
    moves = [(device(i, j, c), device(step(i), j, c)) for i, j, c in PLACES]
    return lax.ppermute(x, "sample", moves)


def over(x, step):
    moves = [(device(i, j, c), device(i, step(j), c)) for i, j, c in PLACES]
    return lax.ppermute(x, "sample", moves)


def swap(x):
    return lax.ppermute(x, "sample", [(i, i ^ 1) for i in range(2 * N * N)])


def unit_kernel(len_ref, emb_ref, out_ref, unit, sem):
    length = len_ref[0]
    lines = lax.broadcasted_iota(jnp.int32, (TAG, unit.shape[1]), 0)
    tag = jnp.where(lines < TAG // 2, length // 16, length % 16)
    unit[LEN : LEN + TAG, :] = tag.astype(jnp.float32).astype(jnp.bfloat16)
    first, stores = None, []
    for n, end in enumerate((HALF, LEN + TAG)):
        start = n * HALF
        values = emb_ref[0, start : start + HALF, :].astype(jnp.float32)
        norm = jnp.sqrt(jnp.sum(values * values, axis=1, keepdims=True) + 1e-06)
        scaled = values / norm
        if first is None:
            first = scaled[0:1, :]
        places = lax.broadcasted_iota(jnp.int32, (HALF, 1), 0) + start
        unit[start : start + HALF, :] = jnp.where(places < length, scaled, first).astype(
            jnp.bfloat16
        )
        store = pltpu.make_async_copy(
            unit.at[start:end, :], out_ref.at[start:end, :], sem.at[n]
        )
        store.start()
        stores.append(store)
    for store in stores:
        store.wait()


def make_unit(lengths, embeddings):
    shape = (LEN + TAG, embeddings.shape[2])
    return pl.pallas_call(
        unit_kernel,
        out_shape=jax.ShapeDtypeStruct(shape, jnp.bfloat16),
        in_specs=[
            pl.BlockSpec(memory_space=pltpu.SMEM),
            pl.BlockSpec(memory_space=pltpu.VMEM),
        ],
        out_specs=pl.BlockSpec(memory_space=pltpu.HBM),
        scratch_shapes=[pltpu.VMEM(shape, jnp.bfloat16), pltpu.SemaphoreType.DMA((2,))],
        compiler_params=pltpu.CompilerParams(vmem_limit_bytes=VMEM),
        name="unit",
    )(lengths, embeddings)


NAMES = (
    "own",
    "near",
    "wide",
    "far",
    "side",
    "next",
    "sib",
    "sib_near",
    "sib_wide",
    "sib_far",
)
SIDE, NEXT, OTHER, ROWS = N, N + 1, 2 * N, 4 * N
FLAGS = ("even", "odd", "inner", "low", "high", "first", "second", "edge")
STAGES = (
    (
        (None, (("near", "sib"), ("wide", "sib"))),
        ("even", (("own", "near"),)),
        ("odd", (("own", "wide"),)),
        ("inner", (("near", "wide"),)),
    ),
    (
        (None, (("far", "sib"), ("far", "sib_near"), ("wide", "sib_near"))),
        ("low", (("side", "own"), ("side", "near"))),
        ("high", (("side", "wide"), ("side", "far"))),
        ("second", (("near", "sib_near"),)),
    ),
    (
        (None, (("far", "sib_wide"),)),
        ("first", (("far", "sib_far"),)),
        ("second", (("wide", "sib_wide"),)),
    ),
    ((None, (("next", "own"), ("next", "near"), ("next", "wide"), ("next", "far"))),),
)


def plan(here):
    core = here % 2
    line, across = (here // 2 % N, here // 2 // N) if core == 0 else (here // 2 // N, here // 2 % N)
    low = across < N // 2
    samples = (
        here,
        device(near(line), across, core),
        device(wide(line), across, core),
        device((line + 2) % N, across, core),
        device(line, wide(across), core),
        device(line, ahead_of(across), core),
        device(across, line, 1 - core),
        device(near(across), line, 1 - core),
        device(wide(across), line, 1 - core),
        device((across + 2) % N, line, 1 - core),
    )
    flags = (line % 2 == 0, line % 2 == 1, line in (1, 2), low, not low, core == 0, core == 1)
    flags += (across in (0, N - 1),)
    rows = (*range(N), SIDE, NEXT, *range(OTHER, OTHER + N))
    return np.array(samples + rows + flags, np.int32)


def make_score(shape, total=2 * N * N):
    owners = lax.broadcasted_iota(jnp.int32, shape, 0)
    lanes = lax.broadcasted_iota(jnp.int32, shape, 1)
    rows = lax.broadcasted_iota(jnp.int32, (LEN, 1), 0).astype(jnp.float32)
    cols = lax.broadcasted_iota(jnp.int32, (1, LEN), 1).astype(jnp.float32)

    def length(tag):
        value = tag.astype(jnp.float32)
        return value[0:1, 0:1] * 16.0 + value[TAG // 2 : TAG // 2 + 1, 0:1]

    def score(row_u, row_v, own, other, both, tok_u, tok_v, tag_u, tag_v):
        len_u, len_v = length(tag_u), length(tag_v)
        similar = lax.dot_general(
            tok_u, tok_v, (((1,), (1,)), ((), ())), preferred_element_type=jnp.float32
        )
        best_row = jnp.max(similar, axis=1, keepdims=True)
        best_col = jnp.max(similar, axis=0, keepdims=True)
        ahead = jnp.sum(jnp.where(rows < len_u, best_row, 0.0), axis=0, keepdims=True)
        behind = jnp.sum(jnp.where(cols < len_v, best_col, 0.0), axis=1, keepdims=True)
        ahead = ahead / len_u
        behind = behind / len_v
        at_u = owners == row_u
        at_v = (owners == row_v) & (both == 1)
        fore = (at_u & (lanes == other)) | (at_v & (lanes == total + own))
        back = (at_u & (lanes == total + other)) | (at_v & (lanes == own))
        return jnp.where(fore, ahead, 0.0) + jnp.where(back, behind, 0.0)

    return score


def first_kernel(here_ref, own_ref, sib_ref, out_ref):
    score = make_score(out_ref.shape)
    here = here_ref[0]
    first = 1 - here % 2
    own, own_tag = own_ref[0:LEN, :], own_ref[LEN : LEN + TAG, 0:128]
    sib, sib_tag = sib_ref[0:LEN, :], sib_ref[LEN : LEN + TAG, 0:128]
    row = jnp.where(first == 1, 0, -1)
    out_ref[...] = score(0, 0, here, here, 0, own, own, own_tag, own_tag) + score(
        row, OTHER, here, here + 1, first, own, sib, own_tag, sib_tag
    )


def run_first(here, own, sib):
    return pl.pallas_call(
        first_kernel,
        out_shape=jax.ShapeDtypeStruct((ROWS, 128), jnp.float32),
        in_specs=[pl.BlockSpec(memory_space=pltpu.SMEM)]
        + [pl.BlockSpec(memory_space=pltpu.VMEM)] * 2,
        out_specs=pl.BlockSpec(memory_space=pltpu.VMEM),
        compiler_params=pltpu.CompilerParams(vmem_limit_bytes=VMEM),
        cost_estimate=pl.CostEstimate(
            flops=4 * LEN * LEN * own.shape[1], bytes_accessed=2 * own.size, transcendentals=0
        ),
        name="pairs_0",
    )(here, own, sib)


def pairs_kernel(stage, names, parts, keep, tab_ref, before_ref, *refs):
    last = stage == len(STAGES) - 1
    given_ref, refs = (refs[0], refs[1:]) if last else (None, refs)
    ins, out_ref = refs[: sum(parts)], refs[sum(parts)]
    score_of = make_score(before_ref.shape)
    blocks, place = {}, 0
    for name, count in zip(names, parts):
        blocks[name] = ins[place : place + count]
        place += count

    if keep:
        refs[-1][...] = blocks[keep][0][...]

    def tokens(name):
        *heads, last = blocks[name]
        rows = LEN - sum(head.shape[0] for head in heads)
        pieces = [head[...] for head in heads] + [last[0:rows, :]]
        pieces = pieces[0] if len(pieces) == 1 else jnp.concatenate(pieces, axis=0)
        return pieces, last[rows : rows + TAG, 0:128]

    def score(pairs):
        result = None
        for u, v in pairs:
            (tok_u, tag_u), (tok_v, tag_v) = tokens(u), tokens(v)
            at, to = NAMES.index(u), NAMES.index(v)
            row_u, row_v = tab_ref[len(NAMES) + at], tab_ref[len(NAMES) + to]
            part = score_of(row_u, row_v, tab_ref[at], tab_ref[to], 1, tok_u, tok_v, tag_u, tag_v)
            result = part if result is None else result + part
        return result

    result = before_ref[...]
    for flag, pairs in STAGES[stage]:
        if last:
            result += score(pairs)
            line = result[0:N] + given_ref[OTHER : OTHER + N, :]
            for k, ref in enumerate(refs[sum(parts) :]):
                row = line[k : k + 1] if k < N else result[NEXT : NEXT + 1]
                ref[...] = jnp.broadcast_to(row, ref.shape)
        elif flag is None:
            out_ref[...] = result + score(pairs)
        else:

            @pl.when(tab_ref[2 * len(NAMES) + FLAGS.index(flag)] == 1)
            def _():
                out_ref[...] += score(pairs)


def run_pairs(stage, table, before, blocks, keep=None, given=()):
    groups = [pair for _, pairs in STAGES[stage] for pair in pairs]
    names = sorted({name for pair in groups for name in pair} | ({keep} if keep else set()))
    chosen = [blocks[name] for name in names]
    chosen = [block if isinstance(block, tuple) else (block,) for block in chosen]
    arrays = [part for block in chosen for part in block]
    width = arrays[0].shape[1]
    hide = stage < 2
    shapes = [(2 * N, 128)] * (N + 1) if given else [before.shape]
    outs = [jax.ShapeDtypeStruct(shape, jnp.float32) for shape in shapes]
    outs += [jax.ShapeDtypeStruct(blocks[keep].shape, jnp.bfloat16)] if keep else []
    return pl.pallas_call(
        functools.partial(pairs_kernel, stage, names, [len(b) for b in chosen], keep),
        out_shape=outs,
        in_specs=[pl.BlockSpec(memory_space=pltpu.SMEM)]
        + [pl.BlockSpec(memory_space=pltpu.VMEM)] * (1 + len(given) + len(arrays)),
        out_specs=[pl.BlockSpec(memory_space=pltpu.VMEM)] * len(outs),
        compiler_params=pltpu.CompilerParams(vmem_limit_bytes=VMEM),
        cost_estimate=pl.CostEstimate(
            flops=2 * len(groups) * LEN * LEN * width if hide else 0,
            bytes_accessed=len(names) * LEN * width * 2 if hide else 0,
            transcendentals=0,
        ),
        name=f"pairs_{stage + 1}",
    )(table, before, *given, *arrays)


def pick_kernel(tab_ref, own_ref, side_ref, out_ref, sem):
    edge = tab_ref[2 * len(NAMES) + FLAGS.index("edge")]
    step = (LEN + TAG) // 3
    for flag, block in ((1, own_ref), (0, side_ref)):

        @pl.when(edge == flag)
        def _():
            copies = []
            for k in range(3):
                rows = pl.ds(k * step, step)
                copies.append(
                    pltpu.make_async_copy(block.at[rows, :], out_ref.at[rows, :], sem.at[k])
                )
            for copy in copies:
                copy.start()
            for copy in copies:
                copy.wait()


def run_pick(table, own, side):
    return pl.pallas_call(
        pick_kernel,
        out_shape=jax.ShapeDtypeStruct(own.shape, own.dtype),
        in_specs=[pl.BlockSpec(memory_space=pltpu.SMEM)]
        + [pl.BlockSpec(memory_space=pl.ANY)] * 2,
        out_specs=pl.BlockSpec(memory_space=pl.ANY),
        scratch_shapes=[pltpu.SemaphoreType.DMA((3,))],
        compiler_params=pltpu.CompilerParams(vmem_limit_bytes=VMEM),
        cost_estimate=pl.CostEstimate(flops=0, bytes_accessed=0, transcendentals=0),
        name="pick",
    )(table, own, side)


def after(x, *others):
    return lax.optimization_barrier((x, *others))[0]


def body(embeddings, lengths):
    total = lax.axis_size("sample")
    here = lax.axis_index("sample")
    blocks = {"own": make_unit(lengths, embeddings)}
    table = jnp.asarray(np.stack([plan(i) for i in range(total)]))[here]
    blocks["wide"] = along(blocks["own"], wide)
    blocks["near"] = along(blocks["own"], near)
    blocks["sib"] = swap(after(blocks["own"], table))
    scores = run_first(here[None], blocks["own"], blocks["sib"])
    blocks["side"] = over(after(blocks["own"], blocks["near"]), wide)
    blocks["far"] = along(blocks["wide"], near)
    blocks["sib_near"] = swap(blocks["near"])
    blocks["sib_wide"] = swap(blocks["wide"])
    (scores,) = run_pairs(0, table, scores, blocks)
    pick = run_pick(table, blocks["own"], after(blocks["side"], scores))
    blocks["next"] = over(pick, near)
    (scores,) = run_pairs(1, table, after(scores, pick), blocks)
    from_side = over(scores, wide)
    far = after(blocks["far"], scores)
    blocks["sib_far"] = (swap(far[:HALF]), swap(far[HALF:]))
    scores, blocks["near"] = run_pairs(2, table, scores, blocks, keep="near")
    mine, *rest = run_pairs(3, table, scores, blocks, given=(swap(scores),))
    result = mine[0] + from_side[SIDE]
    for rows, step in zip(rest, (near, wide, across_from)):
        result += along(rows, step)[0]
    result += over(rest[-1], ahead_of)[0]
    ahead, behind = result[:total], result[total : 2 * total]
    offdiag = jnp.arange(total, dtype=jnp.int32) != here
    utility = jnp.sum(jnp.where(offdiag, ahead + behind, 0.0)) / jnp.float32(2 * (total - 1))
    return ahead[None, :], utility[None]


def solution(mesh):
    in_specs = (P(("prompt", "sample"), None, None), P(("prompt", "sample")))
    out_specs = (P(("prompt", "sample"), None), P(("prompt", "sample")))
    return jax.shard_map(body, mesh=mesh, in_specs=in_specs, out_specs=out_specs, check_vma=False)
```
